128 devices in a mesh: seq: 8 (over x, z_hi), chan: 16 (over y, z_lo, core).
Axes of the slice: x: 4, y: 4, z: 4 (z_hi: 2, z_lo: 2; z = z_hi * 2 + z_lo), core: 2. Of those that a mesh axis runs over, the one named last changes fastest.
Arguments:
- streams: bfloat16 [3, 16384, 8192], P(None, 'seq', 'chan'), may hold values from -6 to 6
- short_taps: float32 [3, 7, 8192], P(None, None, 'chan'), may hold values from -2.4 to 2.4
- rates: float32 [8192, 16], P('chan'), may hold values from 6.1035156e-06 to 0.05, as said below
- residues: float32 [8192, 16], P('chan'), may hold values from -1.5 to 1.5
- out_weight: bfloat16 [8192, 8192], P('chan'), may hold values from -0.09375 to 0.09375
Outputs:
- output: bfloat16 [16384, 8192], P('seq', 'chan')
The draws below stay inside these ranges and needn't reach their ends.
Inputs may be any that keep to these rules, and one draw needn't show every extreme that they name: Every decay rate is positive and at most 0.05, so every mode decays and 1 - exp(-2 rates) is positive.
All inputs are finite; a program needn't handle non-finite values.
Results may differ from the reference program's by a relative error of at most 0.023.
Values may be sent and summed in bfloat16 or wider, within the bound.
A program may use at most 192 MiB of HBM per device.

```python
import math
import jax
import jax.numpy as jnp
from jax import lax

D = 8192
TAPS = 7
MODES = 16
SEQ = 16384
N_CHAN = 16


def draw_rates(key, part):
    key = jax.random.fold_in(key, 11)
    fraction = jax.random.uniform(key, (D, MODES), jnp.float32)
    lowest = 0.2 / SEQ
    highest = 0.05
    return jnp.exp(math.log(lowest) + fraction * (math.log(highest) - math.log(lowest)))


def raised(drawn, stream_key, source, target, blocks, factor):
    def block_of(position):
        return (jnp.arange(drawn.shape[position]) // (drawn.shape[position] // blocks)).reshape((-1,) + (1,) * (drawn.ndim - 1 - position))

    one_side = jax.random.permutation(stream_key, blocks)[block_of(target)]
    second = (block_of(target) + blocks // 2) % blocks
    return jnp.where((block_of(source) == one_side) | (block_of(source) == second), factor * drawn, drawn)


def steps_of(key, dims, cuts, least, high):
    level = 1.0
    for dim, blocks in cuts:
        heights = jax.random.uniform(jax.random.fold_in(jax.random.fold_in(key, 6), dim), (blocks,), jnp.float32, least / len(cuts), high / len(cuts))
        level = level * jnp.repeat(jnp.exp(heights), dims[dim] // blocks).reshape((-1,) + (1,) * (len(dims) - 1 - dim))
    return level


def centred(key, extent, deviation, bound, pieces=(), kind=jnp.bfloat16):
    gain = steps_of(key, extent, pieces, -0.22, 0.18) if pieces else 1.0
    values = jax.random.normal(key, extent, jnp.float32) * deviation * gain
    return jnp.minimum(jnp.maximum(values, -bound), bound).astype(kind)


def gaussian_with(rng, extent, scale, most, cuts, heavy, kind=jnp.bfloat16):
    entries = scale * jax.random.normal(rng, extent, jnp.float32)
    if cuts:
        entries = entries * steps_of(rng, extent, cuts, -0.22, 0.18)
    return jnp.clip(raised(entries, jax.random.fold_in(rng, 3), *heavy), -most, most).astype(kind)


def setup_inputs(seed: int = 0) -> dict:
    key_list = jax.random.split(jax.random.key(seed), 6)
    return {
        "streams": centred(key_list[0], (3, SEQ, D), 1.0, 6.0, ((1, 8), (2, 16))),
        "short_taps": centred(key_list[1], (3, TAPS, D), 0.4, 2.4, ((2, 16),), jnp.float32),
        "rates": draw_rates(jax.random.fold_in(key_list[5], 71), 0),
        "residues": centred(key_list[3], (D, MODES), 0.25, 1.5, ((0, 16),), jnp.float32),
        "out_weight": gaussian_with(key_list[4], (D, D), D ** -0.5, 0.09375, ((0, 16),), (0, 1, 16, 2.0)),
    }


def decayed_prefix(contrib, rates, step):
    nblocks = contrib.shape[0]
    flat = contrib.reshape(nblocks, -1)
    features = flat.shape[1]
    rate_flat = (rates * step).reshape(-1)
    inner = 16 if nblocks > 16 and nblocks % 16 == 0 else nblocks
    outer = nblocks // inner
    lags = (jnp.arange(inner, dtype=jnp.int32)[:, None] - jnp.arange(inner, dtype=jnp.int32)[None, :]).astype(rates.dtype)
    table = jnp.where(lags[:, :, None] >= 0, jnp.exp(-rate_flat[None, None, :] * jnp.maximum(lags, 0.0)[:, :, None]), jnp.zeros((), rates.dtype))
    grid = flat.reshape(outer, inner, features)
    local = jnp.einsum('ijf,gjf->gif', table, grid, precision=lax.Precision.HIGHEST)
    if outer > 1:
        totals = local[:, -1, :]
        glags = (jnp.arange(outer, dtype=jnp.int32)[:, None] - 1 - jnp.arange(outer, dtype=jnp.int32)[None, :]).astype(rates.dtype)
        gtable = jnp.where(glags[:, :, None] >= 0, jnp.exp(-rate_flat[None, None, :] * inner * jnp.maximum(glags, 0.0)[:, :, None]), jnp.zeros((), rates.dtype))
        before = jnp.einsum('ghf,hf->gf', gtable, totals, precision=lax.Precision.HIGHEST)
        steps_in = (jnp.arange(inner, dtype=jnp.int32) + 1).astype(rates.dtype)
        carry_in = jnp.exp(-rate_flat[None, :] * steps_in[:, None])
        local = local + carry_in[None, :, :] * before[:, None, :]
    return local.reshape(contrib.shape)

def block_prefix(values, rates, block_rows):
    row_count, channels = values.shape
    nblocks = row_count // block_rows
    positions = jnp.arange(block_rows).astype(rates.dtype)
    inward = jnp.exp(-rates[:, :, None] * (block_rows - 1 - positions))
    blocks = values.reshape(nblocks, block_rows, channels)
    contrib = jnp.einsum('btc,cmt->bcm', blocks, inward, precision=lax.Precision.HIGHEST)
    return decayed_prefix(contrib, rates, block_rows)

def block_mix(values, rates, residues, block_rows, inclusive, start_state):
    row_count, channels = values.shape
    nblocks = row_count // block_rows
    positions = jnp.arange(block_rows).astype(rates.dtype)
    weights = residues * jnp.sqrt(-jnp.expm1(-2.0 * rates))
    powers = jnp.exp(-rates[:, :, None] * positions)
    kernel = jnp.einsum('cm,cmt->ct', weights, powers, precision=lax.Precision.HIGHEST)
    lag_table = jnp.arange(block_rows, dtype=jnp.int32)[:, None] - jnp.arange(block_rows, dtype=jnp.int32)[None, :]
    toeplitz = jnp.where(lag_table >= 0, kernel[:, jnp.maximum(lag_table, 0)], jnp.zeros((), rates.dtype))
    blocks = values.reshape(nblocks, block_rows, channels)
    intra_part = jnp.einsum('cts,bsc->btc', toeplitz, blocks, precision=lax.Precision.HIGHEST)
    exclusive = jnp.concatenate([jnp.zeros_like(inclusive[:1]), inclusive[:-1]], axis=0)
    block_starts = (jnp.arange(nblocks) * block_rows).astype(rates.dtype)
    offsets = jnp.exp(-rates[None, :, :] * block_starts[:, None, None])
    states = exclusive + offsets * start_state[None]
    outward = weights[:, :, None] * jnp.exp(-rates[:, :, None] * (positions + 1.0))
    inter_part = jnp.einsum('bcm,cmt->btc', states, outward, precision=lax.Precision.HIGHEST)
    return (intra_part + inter_part).reshape(row_count, channels)

def causal_filter(stream, taps):
    tap_count = taps.shape[0]
    margin = tap_count - 1
    length = stream.shape[0]
    padded = jnp.pad(stream.astype(jnp.float32), ((margin, 0), (0, 0)))
    result = jnp.zeros((length, stream.shape[1]), jnp.float32)
    for offset in range(tap_count):
        result = result + taps[offset][None, :] * padded[margin - offset:margin - offset + length]
    return result

def reference(streams, short_taps, rates, residues, out_weight):
    length = streams.shape[1]
    width = streams.shape[2]
    key_conv = causal_filter(streams[1], short_taps[1])
    value_conv = causal_filter(streams[2], short_taps[2])
    product = (key_conv * value_conv).astype(jnp.bfloat16)
    group_width = width // N_CHAN
    groups = width // group_width
    block_rows = min(128, length)
    grouped = product.reshape(length, groups, group_width).transpose(1, 0, 2)
    group_rates = rates.reshape(groups, group_width, MODES)
    group_residues = residues.reshape(groups, group_width, MODES)

    def convolve(items):
        values, item_rates, item_residues = items
        values = values.astype(jnp.float32)
        inclusive = block_prefix(values, item_rates, block_rows)
        zero_state = jnp.zeros((group_width, MODES), jnp.float32)
        return block_mix(values, item_rates, item_residues, block_rows, inclusive, zero_state).astype(jnp.bfloat16)
    mixed = lax.map(convolve, (grouped, group_rates, group_residues))
    mixed = mixed.transpose(1, 0, 2).reshape(length, width)
    query_conv = causal_filter(streams[0], short_taps[0])
    gated = (query_conv * mixed.astype(jnp.float32)).astype(jnp.bfloat16)

    def add_block(accum, index):
        cols = lax.dynamic_slice_in_dim(gated, index * group_width, group_width, 1)
        weight_rows = lax.dynamic_slice_in_dim(out_weight, index * group_width, group_width, 0)
        partial_value = jnp.dot(cols, weight_rows, preferred_element_type=jnp.float32).astype(jnp.bfloat16)
        partial_value = lax.optimization_barrier(partial_value)
        return (accum + partial_value.astype(jnp.float32), None)
    total, _ = lax.scan(add_block, jnp.zeros((length, width), jnp.float32), jnp.arange(N_CHAN, dtype=jnp.int32))
    return total.astype(jnp.bfloat16)
```

```python
import functools

import jax
import jax.numpy as jnp
from jax import lax
from jax.experimental import pallas as pl
from jax.experimental.pallas import tpu as pltpu
from jax.sharding import PartitionSpec as P

MESH = pl.DeviceIdType.MESH
F32 = jnp.float32
BF16 = jnp.bfloat16

TAPS = 7
MODES = 16
ROWS = 2048
WIDTH = 512
LANES = 128
TILES = WIDTH // LANES
CHUNKS = 8
STEPS = ROWS // CHUNKS
WINDOWS = 8
WSTEPS = STEPS // WINDOWS
WROWS = ROWS // WINDOWS
HALF = WIDTH // 2
PAD = 8
ORDER = (2, 1, 3, 0)
SEQ = 8
XPART = WIDTH // 4

LAG_F, LAG_2, LAG_1, LAG_0 = 2, 2, 3, 5


def kernel(
    streams, taps, rates, gains, weight, out,
    sbuf, halo, nat, prod, query, state, decay, gain, total, totals, stage,
    gated, wbuf, relay_out, relay_in, side_out, side_in, result,
    load_sem, wown_sem, halo_sem, state_sem, wsib_sem, wz_sem, wx1_sem, wx2_sem,
    gz_sem, gs_sem, gf_sem, relay_sem, side_sem, result_sem,
):
    seq, chan = lax.axis_index("seq"), lax.axis_index("chan")
    x, zh = lax.div(seq, 2), lax.rem(seq, 2)
    y, zl, core = lax.div(chan, 4), lax.rem(lax.div(chan, 2), 2), lax.rem(chan, 2)
    mine = zl * 2 + core
    sib_chan = chan + 1 - 2 * core
    z_chan = chan + 2 - 4 * zl

    def chan_of(yy, zz, cc):
        return (yy * 2 + zz) * 2 + cc

    def y_off(k):
        return lax.rem(y + k, 4)

    sibling = (seq, sib_chan)
    z_near = (seq, z_chan)
    zh_seq = seq + 1 - 2 * zh
    z_far = tuple((zh_seq, chan_of(y, 1 - zl, c)) for c in range(2))
    y_up = (seq, chan_of(y_off(1), zl, core))
    y_down = (seq, chan_of(y_off(3), zl, core))
    x_up = (lax.rem(seq + 2, SEQ), chan)
    x_down = (lax.rem(seq + 6, SEQ), chan)
    seq_of = lambda k: (lax.rem(seq + k, SEQ), chan)

    def send(src, dst, sems, index, device):
        return pltpu.make_async_remote_copy(
            src_ref=src, dst_ref=dst, send_sem=sems.at[(0, *index)], recv_sem=sems.at[(1, *index)],
            device_id=device, device_id_type=MESH,
        )

    def load(j):
        return pltpu.make_async_copy(streams.at[j], sbuf.at[j], load_sem.at[j])

    def columns(block, zz, cc):
        return pl.ds(pl.multiple_of(chan_of(y_off(block), zz, cc) * WIDTH, WIDTH), WIDTH)

    def own_weight(block):
        rows = pl.ds(pl.multiple_of(mine * WIDTH, WIDTH), WIDTH)
        return pltpu.make_async_copy(
            weight.at[:, columns(block, zl, core)], wbuf.at[block, rows], wown_sem.at[block]
        )

    for j in (1, 2, 0):
        load(j).start()
    for block in ORDER:
        own_weight(block).start()

    barrier = pltpu.get_barrier_semaphore()
    partners = [seq_of(k) for k in range(1, SEQ)] + [sibling, z_near, *z_far, y_up, y_down]
    for device in partners:
        pl.semaphore_signal(barrier, inc=1, device_id=device, device_id_type=MESH)
    pl.semaphore_wait(barrier, len(partners))

    halo_copy = send(streams.at[:, pl.ds(ROWS - 16, 16)], halo, halo_sem, (), seq_of(1))
    halo_copy.start()

    def weight_far_from(block, c):
        rows = pl.ds(pl.multiple_of((2 - 2 * zl + c) * WIDTH + x * XPART, XPART), XPART)
        return send(wbuf.at[block, rows], wbuf.at[block, rows], wz_sem, (block, c), z_far[0])

    def weight_sib(block):
        rows = pl.ds(pl.multiple_of(mine * WIDTH, WIDTH), WIDTH)
        return send(
            weight.at[:, columns(block, zl, 1 - core)], wbuf.at[block, rows], wsib_sem, (block,), sibling
        )

    def weight_x(block, c, part, device, sems, index):
        rows = pl.ds(pl.multiple_of((2 - 2 * zl + c) * WIDTH + part * XPART, XPART), XPART)
        return send(wbuf.at[block, rows], wbuf.at[block, rows], sems, index, device)

    def weight_x1(block):
        return [
            weight_x(block, c, x, device, wx1_sem, (block, way, c))
            for c in range(2)
            for way, device in enumerate((x_up, x_down))
        ]

    def weight_x2(block):
        return [
            weight_x(block, 0, lax.rem(x + 3, 4), x_up, wx2_sem, (block, 0)),
            weight_x(block, 1, lax.rem(x + 1, 4), x_down, wx2_sem, (block, 1)),
        ]

    for block in ORDER:
        for c in range(2):
            rows = pl.ds(pl.multiple_of(mine * WIDTH + x * XPART, XPART), XPART)
            part = pl.ds(pl.multiple_of(x * XPART, XPART), XPART)
            pltpu.make_async_remote_copy(
                src_ref=weight.at[part, columns(block, 1 - zl, c)], dst_ref=wbuf.at[block, rows],
                send_sem=wz_sem.at[0, block, c], recv_sem=wz_sem.at[1, block, core],
                device_id=z_far[c], device_id_type=MESH,
            ).start()
        weight_sib(block).start()

    def pass_x1(block):
        for c in range(2):
            weight_far_from(block, c).wait_recv()
        for copy in weight_x1(block):
            copy.start()

    def pass_x2(block):
        for copy in weight_x1(block):
            copy.wait_recv()
        for copy in weight_x2(block):
            copy.start()

    def have_weight(block):
        for copy in weight_x2(block):
            copy.wait_recv()
        weight_sib(block).wait_recv()
        own_weight(block).wait()

    def lanes_of(tile):
        return pl.ds(pl.multiple_of(tile * LANES, LANES), LANES)

    @pl.loop(0, TILES)
    def _(tile):
        for m in range(MODES):
            rate = rates[pl.ds(m, 1), lanes_of(tile)]
            decay[tile, m] = jnp.broadcast_to(jnp.exp(-rate), (CHUNKS, LANES))
            gain[tile, m] = jnp.broadcast_to(gains[pl.ds(m, 1), lanes_of(tile)], (CHUNKS, LANES))

    first = jnp.where(seq > 0, 1.0, 0.0).astype(F32)

    def widen(j, tile, slot):
        lanes = lanes_of(tile)
        nat[slot, pl.ds(0, PAD)] = halo[j, :, lanes].astype(F32)[16 - PAD :] * first

        @pl.loop(0, ROWS // 128)
        def _(i):
            row = pl.multiple_of(i * 128, 128)
            nat[slot, pl.ds(pl.multiple_of(row + PAD, PAD), 128)] = sbuf[j, pl.ds(row, 128), lanes].astype(F32)

    def across(slot, step):
        return nat[slot, pl.ds(PAD + step, CHUNKS, stride=STEPS), :]

    def filtered(window, coefs):
        terms = [c * v for c, v in zip(coefs, window, strict=True)]
        while len(terms) > 1:
            terms = [a + b for a, b in zip(terms[::2], terms[1::2])] + ([terms[-1]] if len(terms) % 2 else [])
        return terms[0]

    def coefs_of(j, tile):
        return [
            jnp.broadcast_to(taps[j, pl.ds(i, 1), lanes_of(tile)], (CHUNKS, LANES)) for i in range(TAPS)
        ]

    def convolve(tile, pairs, target):
        coefs = [coefs_of(j, tile) for j, _ in pairs]
        before = [tuple(across(slot, -i) for i in range(1, TAPS)) for _, slot in pairs]

        def body(g, before):
            before = list(before)
            for u in range(8):
                step = g * 8 + u
                value = None
                for k, (_, slot) in enumerate(pairs):
                    window = (across(slot, step), *before[k])
                    part = filtered(window, coefs[k])
                    value = part if value is None else value * part
                    before[k] = window[:-1]
                target[tile, pl.ds(pl.multiple_of(step * CHUNKS, CHUNKS), CHUNKS)] = value
            return tuple(before)

        lax.fori_loop(0, STEPS // 8, body, tuple(before))

    load(1).wait()
    load(2).wait()
    halo_copy.wait_recv()

    @pl.loop(0, TILES)
    def _(tile):
        widen(1, tile, 0)
        widen(2, tile, 1)
        convolve(tile, ((1, 0), (2, 1)), prod)

    pass_x1(ORDER[0])

    sublane = lax.broadcasted_iota(jnp.int32, (CHUNKS, LANES), 0)

    @pl.loop(0, TILES)
    def _(tile):
        decays = [decay[tile, m] for m in range(MODES)]

        def body(g, states):
            states = list(states)
            for u in range(8):
                step = pl.multiple_of((g * 8 + u) * CHUNKS, CHUNKS)
                value = prod[tile, pl.ds(step, CHUNKS)]
                states = [a * s + value for a, s in zip(decays, states)]
            return tuple(states)

        zero = jnp.zeros((CHUNKS, LANES), F32)
        ends = lax.fori_loop(0, STEPS // 8, body, (zero,) * MODES)
        for m in range(MODES):
            rate = jnp.broadcast_to(rates[pl.ds(m, 1), lanes_of(tile)], (CHUNKS, LANES))
            run = ends[m]
            for shift in (1, 2, 4):
                moved = jnp.where(sublane >= shift, pltpu.roll(run, shift, 0), 0.0)
                run = run + jnp.exp(-rate * float(STEPS * shift)) * moved
            state[tile, m] = jnp.where(sublane >= 1, pltpu.roll(run, 1, 0), 0.0)
            total[pl.ds(m, 1), lanes_of(tile)] = run[CHUNKS - 1 :]

    def state_copy(k):
        return send(total, totals.at[k], state_sem, (k,), seq_of(k))

    for k in range(1, SEQ):
        state_copy(k).start()

    pass_x1(ORDER[1])

    load(0).wait()

    @pl.loop(0, TILES)
    def _(tile):
        widen(0, tile, 0)
        convolve(tile, ((0, 0),), query)

    pass_x2(ORDER[0])
    pass_x1(ORDER[2])

    for k in range(1, SEQ):
        state_copy(k).wait_recv()

    @pl.loop(0, TILES)
    def _(tile):
        lanes = lanes_of(tile)
        rate = rates[:, lanes]
        start = jnp.zeros((MODES, LANES), F32)
        for k in range(1, SEQ):
            part = jnp.exp(-rate * float(ROWS * (k - 1))) * totals[k, :, lanes]
            start = start + jnp.where(seq >= k, part, 0.0)
        for m in range(MODES):
            spread = jnp.broadcast_to(rate[m : m + 1], (CHUNKS, LANES)) * (sublane * STEPS).astype(F32)
            state[tile, m] = state[tile, m] + jnp.exp(-spread) * start[m : m + 1]

    def own_lanes():
        return pl.ds(pl.multiple_of(mine * WIDTH, WIDTH), WIDTH)

    def part_of(w, source):
        return gated.at[w, :, pl.ds(pl.multiple_of(source * WIDTH, WIDTH), WIDTH)]

    def to_near(w):
        return send(part_of(w, mine), part_of(w, mine), gz_sem, (w,), z_near)

    def to_sibling(w):
        return send(part_of(w, mine), part_of(w, mine), gs_sem, (w,), sibling)

    def forward(w):
        source = (1 - zl) * 2 + core
        return send(part_of(w, source), part_of(w, source), gf_sem, (w,), sibling)

    def make_gated(w):
        @pl.loop(0, TILES)
        def _(tile):
            decays = [decay[tile, m] for m in range(MODES)]
            weights = [gain[tile, m] for m in range(MODES)]

            def body(g, states):
                states = list(states)
                for u in range(8):
                    at = g * 8 + u
                    row = pl.ds(pl.multiple_of((w * WSTEPS + at) * CHUNKS, CHUNKS), CHUNKS)
                    value = prod[tile, row]
                    states = [a * s + value for a, s in zip(decays, states)]
                    mixed = filtered(states, weights)
                    stage[pl.ds(at, CHUNKS, stride=WSTEPS), :] = mixed * query[tile, row]
                return tuple(states)

            states = lax.fori_loop(0, WSTEPS // 8, body, tuple(state[tile, m] for m in range(MODES)))
            for m in range(MODES):
                state[tile, m] = states[m]
            lanes = pl.ds(pl.multiple_of(mine * WIDTH + tile * LANES, LANES), LANES)
            gated[w, :, lanes] = stage[...].astype(BF16)

        to_near(w).start()
        to_sibling(w).start()

    def dot(w, block, n):
        return jnp.dot(gated[w], wbuf[block, :, pl.ds(n * HALF, HALF)], preferred_element_type=F32)

    ups = (y_up, y_down)

    def relay(w, way):
        return send(relay_out.at[way, w], relay_in.at[way, w], relay_sem, (way, w), ups[way])

    def side(w, way, n):
        return send(side_out.at[way, w, n], side_in.at[way, w, n], side_sem, (way, w, n), ups[way])

    def store(w, n):
        rows = pl.ds(pl.multiple_of(w * WSTEPS, WSTEPS), WSTEPS)
        return pltpu.make_async_copy(
            result.at[w, n], out.at[:, rows, pl.ds(n * HALF, HALF)], result_sem.at[w, n]
        )

    def opposite(w):
        for way in range(2):
            relay_out[way, w] = dot(w, 2, way).astype(BF16)
            relay(w, way).start()

    def sides(w):
        for way, block in ((0, 1), (1, 3)):
            side_out[way, w, 1 - way] = dot(w, block, 1 - way).astype(BF16)
            side(w, way, 1 - way).start()
        for way, block in ((0, 1), (1, 3)):
            part = dot(w, block, way)
            relay(w, way).wait_recv()
            side_out[way, w, way] = (part + relay_in[way, w].astype(F32)).astype(BF16)
            side(w, way, way).start()

    def finish(w):
        for n in range(2):
            part = dot(w, 0, n)
            for way in range(2):
                side(w, way, n).wait_recv()
                part = part + side_in[way, w, n].astype(F32)
            result[w, n] = part.astype(BF16).reshape(CHUNKS, WSTEPS, HALF)
            store(w, n).start()

    @pl.loop(0, WINDOWS + LAG_0)
    def _(i):
        @pl.when((i >= LAG_F) & (i < WINDOWS + LAG_F))
        def _():
            w = i - LAG_F
            to_near(w).wait_recv()
            forward(w).start()

        @pl.when(i < WINDOWS)
        def _():
            make_gated(i)

        @pl.when(i == 0)
        def _():
            pass_x2(ORDER[1])
            pass_x1(ORDER[3])

        @pl.when(i == 1)
        def _():
            pass_x2(ORDER[2])

        @pl.when(i == 2)
        def _():
            have_weight(ORDER[0])

        @pl.when(i == 3)
        def _():
            pass_x2(ORDER[3])
            have_weight(ORDER[1])
            have_weight(ORDER[2])

        @pl.when(i == LAG_0)
        def _():
            have_weight(ORDER[3])

        @pl.when((i >= LAG_2) & (i < WINDOWS + LAG_2))
        def _():
            w = i - LAG_2
            to_sibling(w).wait_recv()
            forward(w).wait_recv()
            opposite(w)

        @pl.when((i >= LAG_1) & (i < WINDOWS + LAG_1))
        def _():
            sides(i - LAG_1)

        @pl.when(i >= LAG_0)
        def _():
            finish(i - LAG_0)

    halo_copy.wait_send()
    for k in range(1, SEQ):
        state_copy(k).wait_send()
    for block in ORDER:
        for c in range(2):
            pltpu.make_async_remote_copy(
                src_ref=weight.at[pl.ds(0, XPART), columns(block, 1 - zl, c)],
                dst_ref=wbuf.at[block, pl.ds(0, XPART)],
                send_sem=wz_sem.at[0, block, c], recv_sem=wz_sem.at[1, block, c],
                device_id=z_far[c], device_id_type=MESH,
            ).wait_send()
        weight_sib(block).wait_send()
        for copy in weight_x1(block) + weight_x2(block):
            copy.wait_send()

    @pl.loop(0, WINDOWS)
    def _(w):
        to_near(w).wait_send()
        to_sibling(w).wait_send()
        forward(w).wait_send()
        for way in range(2):
            relay(w, way).wait_send()
            for n in range(2):
                side(w, way, n).wait_send()
        for n in range(2):
            store(w, n).wait()


def on_device(streams, short_taps, rates, residues, out_weight):
    gains = residues * jnp.sqrt(-jnp.expm1(-2.0 * rates))
    dma = pltpu.SemaphoreType.DMA
    vmem = pl.BlockSpec(memory_space=pltpu.VMEM)
    hbm = pl.BlockSpec(memory_space=pl.ANY)
    result = pl.pallas_call(
        kernel,
        out_shape=jax.ShapeDtypeStruct((CHUNKS, STEPS, WIDTH), BF16),
        in_specs=[hbm, vmem, vmem, vmem, hbm],
        out_specs=hbm,
        scratch_shapes=[
            pltpu.VMEM((3, ROWS, WIDTH), BF16),
            pltpu.VMEM((3, 16, WIDTH), BF16),
            pltpu.VMEM((2, ROWS + PAD, LANES), F32),
            pltpu.VMEM((TILES, ROWS, LANES), F32),
            pltpu.VMEM((TILES, ROWS, LANES), F32),
            pltpu.VMEM((TILES, MODES, CHUNKS, LANES), F32),
            pltpu.VMEM((TILES, MODES, CHUNKS, LANES), F32),
            pltpu.VMEM((TILES, MODES, CHUNKS, LANES), F32),
            pltpu.VMEM((MODES, WIDTH), F32),
            pltpu.VMEM((SEQ, MODES, WIDTH), F32),
            pltpu.VMEM((WROWS, LANES), F32),
            pltpu.VMEM((WINDOWS, WROWS, 4 * WIDTH), BF16),
            pltpu.VMEM((4, 4 * WIDTH, WIDTH), BF16),
            pltpu.VMEM((2, WINDOWS, WROWS, HALF), BF16),
            pltpu.VMEM((2, WINDOWS, WROWS, HALF), BF16),
            pltpu.VMEM((2, WINDOWS, 2, WROWS, HALF), BF16),
            pltpu.VMEM((2, WINDOWS, 2, WROWS, HALF), BF16),
            pltpu.VMEM((WINDOWS, 2, CHUNKS, WSTEPS, HALF), BF16),
            dma((3,)),
            dma((4,)),
            dma((2,)),
            dma((2, SEQ)),
            dma((2, 4)),
            dma((2, 4, 2)),
            dma((2, 4, 2, 2)),
            dma((2, 4, 2)),
            dma((2, WINDOWS)),
            dma((2, WINDOWS)),
            dma((2, WINDOWS)),
            dma((2, 2, WINDOWS)),
            dma((2, 2, WINDOWS, 2)),
            dma((WINDOWS, 2)),
        ],
        compiler_params=pltpu.CompilerParams(
            collective_id=0, has_side_effects=True, vmem_limit_bytes=60 * 1024 * 1024
        ),
        cost_estimate=pl.CostEstimate(
            flops=2 * ROWS * WIDTH * 8192, bytes_accessed=16 * 1024 * 1024, transcendentals=0
        ),
        name="mixer",
    )(streams, short_taps, rates.T, gains.T, out_weight)
    return result.reshape(ROWS, WIDTH)


def solution(mesh):
    return jax.shard_map(
        on_device,
        mesh=mesh,
        in_specs=(
            P(None, "seq", "chan"),
            P(None, None, "chan"),
            P("chan", None),
            P("chan", None),
            P("chan", None),
        ),
        out_specs=P("seq", "chan"),
        check_vma=False,
    )
```

```python
import functools

import jax
import jax.numpy as jnp
from jax import lax
from jax.experimental import pallas as pl
from jax.experimental.pallas import tpu as pltpu
from jax.sharding import PartitionSpec as P

MESH = pl.DeviceIdType.MESH
F32 = jnp.float32
BF16 = jnp.bfloat16

TAPS = 7
MODES = 16
ROWS = 2048
WIDTH = 512
LANES = 128
TILES = WIDTH // LANES
CHUNKS = 8
STEPS = ROWS // CHUNKS
WINDOWS = 16
WSTEPS = STEPS // WINDOWS
WROWS = ROWS // WINDOWS
HALF = WIDTH // 2
UNROLL = 16
EARLY = 8
PAD = 8
PITCH = STEPS + PAD
SPITCH = WSTEPS + PAD
PIECES = (((2, None),), ((1, 1), (3, 0)), ((1, 0), (3, 1)), ((0, None),))
SEQ = 8
XPART = WIDTH // 4

LAG_F, LAG_2, LAG_1, LAG_0 = 2, 3, 5, 8


def kernel(
    streams, taps_in, rates_in, gains_in, weight, out,
    taps, rates, gains,
    sbuf, halo, nat, prod, query, state, decay, gain, total, totals, stage,
    gated, wbuf, relay_out, relay_in, side_out, side_in, result,
    small_sem, load_sem, out_sem, wown_sem, halo_sem, state_sem, wsib_sem, wz_sem, wx_sem,
    gz_sem, gs_sem, relay_sem, side_sem, result_sem,
):
    seq, chan = lax.axis_index("seq"), lax.axis_index("chan")
    x, zh = lax.div(seq, 2), lax.rem(seq, 2)
    y, zl, core = lax.div(chan, 4), lax.rem(lax.div(chan, 2), 2), lax.rem(chan, 2)
    mine = zl * 2 + core
    sib_chan = chan + 1 - 2 * core
    z_chan = chan + 2 - 4 * zl

    def chan_of(yy, zz, cc):
        return (yy * 2 + zz) * 2 + cc

    def y_off(k):
        return lax.rem(y + k, 4)

    sibling = (seq, sib_chan)
    z_near = (seq, z_chan)
    near = tuple((seq, chan_of(y, 1 - zl, c)) for c in range(2))
    zh_seq = seq + 1 - 2 * zh
    z_far = tuple((zh_seq, chan_of(y, 1 - zl, c)) for c in range(2))
    y_up = (seq, chan_of(y_off(1), zl, core))
    y_down = (seq, chan_of(y_off(3), zl, core))
    x_up = (lax.rem(seq + 2, SEQ), chan)
    x_down = (lax.rem(seq + 6, SEQ), chan)
    seq_of = lambda k: (lax.rem(seq + k, SEQ), chan)

    (HALO, STATE, WSIB, WZ, WX, NEAR, SIB, RELAY, SIDE) = range(9)

    def send(src, dst, kind, sem, device):
        return pltpu.make_async_remote_copy(
            src_ref=src, dst_ref=dst, send_sem=out_sem.at[kind], recv_sem=sem,
            device_id=device, device_id_type=MESH,
        )

    def arrived(ref, sem):
        send(ref, ref, 0, sem, sibling).wait_recv()

    def left(ref, kind):
        send(ref, ref, kind, halo_sem.at[0], sibling).wait_send()

    small = [
        pltpu.make_async_copy(a, b, small_sem.at[i])
        for i, (a, b) in enumerate(((rates_in, rates), (gains_in, gains), (taps_in, taps)))
    ]

    def load(j, tile):
        lanes = pl.ds(pl.multiple_of(tile * LANES, LANES), LANES)
        return pltpu.make_async_copy(streams.at[j, :, lanes], sbuf.at[j, :, lanes], load_sem.at[j, tile])

    def columns(block, n, zz, cc):
        first = chan_of(y_off(block), zz, cc) * WIDTH
        if n is None:
            return pl.ds(pl.multiple_of(first, WIDTH), WIDTH)
        return pl.ds(pl.multiple_of(first + n * HALF, HALF), HALF)

    def half(n):
        return slice(None) if n is None else pl.ds(n * HALF, HALF)

    def own_weight(block):
        return pltpu.make_async_copy(
            weight.at[:, columns(block, None, zl, core)], wbuf.at[block, mine], wown_sem.at[block]
        )

    barrier = pltpu.get_barrier_semaphore()
    partners = [seq_of(k) for k in range(1, SEQ)] + [sibling, *near, *z_far, y_up, y_down]
    for device in partners:
        pl.semaphore_signal(barrier, inc=1, device_id=device, device_id_type=MESH)
    for copy in small:
        copy.start()
    for tile in range(TILES):
        for j in (1, 2):
            load(j, tile).start()

    halo_copy = send(streams.at[:, pl.ds(ROWS - 16, 16)], halo, HALO, halo_sem.at[0], seq_of(1))

    pair = 2 * lax.rem(x, 2)
    far_sources = pl.ds(2 - 2 * zl, 2)

    def part_rows(part):
        return pl.ds(pl.multiple_of(part * XPART, XPART), XPART)

    def start_weight(piece):
        for block, n in PIECES[piece]:
            for link in range(2):
                chip = near if link == 1 and piece < 2 else z_far
                for c in range(2):
                    send(
                        weight.at[part_rows(pair + link), columns(block, n, 1 - zl, c)],
                        wbuf.at[block, mine, part_rows(pair + link), half(n)],
                        WZ, wz_sem.at[piece], chip[c],
                    ).start()

    def pass_weight(piece):
        arrived(wbuf.at[0, 0], wz_sem.at[piece])
        for block, n in PIECES[piece]:
            for way, device in enumerate((x_up, x_down)):
                there = wbuf.at[block, far_sources, part_rows(pair + way), half(n)]
                send(there, there, WX, wx_sem.at[piece], device).start()

    def have_weight(piece):
        arrived(wbuf.at[0, 0], wx_sem.at[piece])

    def near_weight(block):
        there = wbuf.at[block, mine]
        return send(weight.at[:, columns(block, None, zl, 1 - core)], there, WSIB, wsib_sem.at[block], sibling)

    def have_near_weight(block):
        arrived(wbuf.at[block, 0], wsib_sem.at[block])
        own_weight(block).wait()

    pl.semaphore_wait(barrier, len(partners))
    halo_copy.start()
    start_weight(0)
    for copy in small:
        copy.wait()

    def lanes_of(tile):
        return pl.ds(pl.multiple_of(tile * LANES, LANES), LANES)

    @pl.loop(0, TILES)
    def _(tile):
        for m in range(MODES):
            rate = rates[pl.ds(m, 1), lanes_of(tile)]
            decay[tile, m] = jnp.broadcast_to(jnp.exp(-rate), (CHUNKS, LANES))
            gain[tile, m] = jnp.broadcast_to(gains[pl.ds(m, 1), lanes_of(tile)], (CHUNKS, LANES))

    first = jnp.where(seq > 0, 1.0, 0.0).astype(F32)

    def edge(j, tile, slot):
        nat[slot, pl.ds(0, PAD)] = halo[j, :, lanes_of(tile)].astype(F32)[16 - PAD :] * first

    def widen(j, tile, slot):
        lanes = lanes_of(tile)
        nat[slot, pl.ds(PAD, STEPS)] = sbuf[j, pl.ds(0, STEPS), lanes].astype(F32)

        @pl.loop(1, CHUNKS)
        def _(c):
            row = pl.multiple_of(c * STEPS - 16, 16)
            to = pl.multiple_of(c * PITCH, PAD)
            nat[slot, pl.ds(to, PITCH)] = sbuf[j, pl.ds(row, STEPS + 16), lanes].astype(F32)[16 - PAD :]

    def across(slot, step):
        return nat[slot, pl.ds(PAD + step, CHUNKS, stride=PITCH), :]

    def filtered(window, coefs):
        terms = [c * v for c, v in zip(coefs, window, strict=True)]
        while len(terms) > 1:
            terms = [a + b for a, b in zip(terms[::2], terms[1::2])] + ([terms[-1]] if len(terms) % 2 else [])
        return terms[0]

    def coefs_of(j, tile):
        return [
            jnp.broadcast_to(taps[j, pl.ds(i, 1), lanes_of(tile)], (CHUNKS, LANES)) for i in range(TAPS)
        ]

    def convolve(tile, pairs, target, first_group, groups):
        coefs = [coefs_of(j, tile) for j, _ in pairs]
        before = [tuple(across(slot, first_group * 8 - i) for i in range(1, TAPS)) for _, slot in pairs]

        def body(g, before):
            before = list(before)
            for u in range(8):
                step = g * 8 + u
                value = None
                for k, (_, slot) in enumerate(pairs):
                    window = (across(slot, step), *before[k])
                    part = filtered(window, coefs[k])
                    value = part if value is None else value * part
                    before[k] = window[:-1]
                target[tile, pl.ds(pl.multiple_of(step * CHUNKS, CHUNKS), CHUNKS)] = value
            return tuple(before)

        lax.fori_loop(first_group, groups, body, tuple(before))

    @pl.loop(0, TILES)
    def _(tile):
        load(1, tile).wait()
        load(2, tile).wait()
        widen(1, tile, 2 * tile)
        widen(2, tile, 2 * tile + 1)

        for slot in range(2):
            nat[2 * tile + slot, pl.ds(0, PAD)] = jnp.zeros((PAD, LANES), F32)
        convolve(tile, ((1, 2 * tile), (2, 2 * tile + 1)), prod, 0, STEPS // 8)

        @pl.when(tile == 2)
        def _():
            start_weight(1)
            for block in (2, 1, 3, 0):
                near_weight(block).start()
                own_weight(block).start()

    for tile in range(TILES):
        load(0, tile).start()
    arrived(halo, halo_sem.at[0])

    @pl.loop(0, TILES)
    def _(tile):
        edge(1, tile, 2 * tile)
        edge(2, tile, 2 * tile + 1)
        convolve(tile, ((1, 2 * tile), (2, 2 * tile + 1)), prod, 0, 1)

    sublane = lax.broadcasted_iota(jnp.int32, (CHUNKS, LANES), 0)

    @pl.loop(0, TILES)
    def _(tile):
        decays = [decay[tile, m] for m in range(MODES)]

        def body(g, states):
            states = list(states)
            for u in range(8):
                step = pl.multiple_of((g * 8 + u) * CHUNKS, CHUNKS)
                value = prod[tile, pl.ds(step, CHUNKS)]
                states = [a * s + value for a, s in zip(decays, states)]
            return tuple(states)

        zero = jnp.zeros((CHUNKS, LANES), F32)
        ends = lax.fori_loop(0, STEPS // 8, body, (zero,) * MODES)
        for m in range(MODES):
            rate = jnp.broadcast_to(rates[pl.ds(m, 1), lanes_of(tile)], (CHUNKS, LANES))
            run = ends[m]
            for shift in (1, 2, 4):
                moved = jnp.where(sublane >= shift, pltpu.roll(run, shift, 0), 0.0)
                run = run + jnp.exp(-rate * float(STEPS * shift)) * moved
            state[tile, m] = jnp.where(sublane >= 1, pltpu.roll(run, 1, 0), 0.0)
            total[pl.ds(m, 1), lanes_of(tile)] = run[CHUNKS - 1 :]

        @pl.when(tile == 0)
        def _():
            pass_weight(0)

        @pl.when(tile == 1)
        def _():
            start_weight(2)

    for k in range(1, SEQ):
        send(total, totals.at[k], STATE, state_sem.at[k], seq_of(k)).start()

    @pl.loop(0, TILES)
    def _(tile):
        load(0, tile).wait()
        widen(0, tile, tile)
        edge(0, tile, tile)
        convolve(tile, ((0, tile),), query, 0, EARLY)

    pass_weight(1)
    start_weight(3)
    for k in range(1, SEQ):
        arrived(totals.at[k], state_sem.at[k])

    @pl.loop(0, TILES)
    def _(tile):
        lanes = lanes_of(tile)
        rate = rates[:, lanes]
        start = jnp.zeros((MODES, LANES), F32)
        for k in range(1, SEQ):
            part = jnp.exp(-rate * float(ROWS * (k - 1))) * totals[k, :, lanes]
            start = start + jnp.where(seq >= k, part, 0.0)
        for m in range(MODES):
            spread = jnp.broadcast_to(rate[m : m + 1], (CHUNKS, LANES)) * (sublane * STEPS).astype(F32)
            state[tile, m] = state[tile, m] + jnp.exp(-spread) * start[m : m + 1]

    def own_lanes():
        return pl.ds(pl.multiple_of(mine * WIDTH, WIDTH), WIDTH)

    def part_of(w, source):
        return gated.at[w, :, pl.ds(pl.multiple_of(source * WIDTH, WIDTH), WIDTH)]

    def to_near(w):
        return send(part_of(w, mine), part_of(w, mine), NEAR, gz_sem.at[w], z_near)

    def to_sibling(w):
        return send(part_of(w, mine), part_of(w, mine), SIB, gs_sem.at[w], sibling)

    def forward(w):
        source = (1 - zl) * 2 + core
        arrived(part_of(w, source), gz_sem.at[w])
        return send(part_of(w, source), part_of(w, source), SIB, gs_sem.at[w], sibling)

    def make_gated(w):
        @pl.loop(0, TILES)
        def _(tile):
            decays = [decay[tile, m] for m in range(MODES)]
            weights = [gain[tile, m] for m in range(MODES)]

            def body(g, states):
                states = list(states)
                for u in range(UNROLL):
                    at = g * UNROLL + u
                    row = pl.ds(pl.multiple_of((w * WSTEPS + at) * CHUNKS, CHUNKS), CHUNKS)
                    value = prod[tile, row]
                    states = [a * s + value for a, s in zip(decays, states)]
                    mixed = filtered(states, weights)
                    stage[pl.ds(at, CHUNKS, stride=SPITCH), :] = mixed * query[tile, row]
                return tuple(states)

            states = lax.fori_loop(0, WSTEPS // UNROLL, body, tuple(state[tile, m] for m in range(MODES)))
            for m in range(MODES):
                state[tile, m] = states[m]
            lanes = pl.ds(pl.multiple_of(mine * WIDTH + tile * LANES, LANES), LANES)
            for c in range(CHUNKS):
                rows = pl.ds(c * WSTEPS, WSTEPS)
                gated[w, rows, lanes] = stage[pl.ds(c * SPITCH, WSTEPS)].astype(BF16)

        to_near(w).start()
        to_sibling(w).start()

    def dot(w, block, n):
        columns = wbuf[block, :, :, half(n)]
        return jnp.dot(gated[w], columns.reshape(4 * WIDTH, -1), preferred_element_type=F32)

    ups = (y_up, y_down)

    def side(w, way, n):
        return send(side_out.at[way, w, n], side_in.at[way, w, n], SIDE, side_sem.at[w], ups[way])

    def store(w):
        rows = pl.ds(pl.multiple_of(w * WSTEPS, WSTEPS), WSTEPS)
        return pltpu.make_async_copy(result.at[w], out.at[:, rows], result_sem.at[0])

    def opposite(w):
        part = dot(w, 2, None).astype(BF16)
        for way in range(2):
            relay_out[way, w] = part[:, way * HALF : (way + 1) * HALF]
        for way in range(2):
            send(relay_out.at[way, w], relay_in.at[way, w], RELAY, relay_sem.at[w], ups[way]).start()

    def sides_own(w):
        parts = [dot(w, block, 1 - way).astype(BF16) for way, block in ((0, 1), (1, 3))]
        for way in range(2):
            side_out[way, w, 1 - way] = parts[way]
        for way in range(2):
            side(w, way, 1 - way).start()

    def sides_relayed(w):
        parts = [dot(w, block, way) for way, block in ((0, 1), (1, 3))]
        arrived(relay_in.at[:, w], relay_sem.at[w])
        for way in range(2):
            side_out[way, w, way] = (parts[way] + relay_in[way, w].astype(F32)).astype(BF16)
        for way in range(2):
            side(w, way, way).start()

    def finish(w):
        part = dot(w, 0, None)
        arrived(side_in.at[:, w], side_sem.at[w])
        for n in range(2):
            sides = side_in[0, w, n].astype(F32) + side_in[1, w, n].astype(F32)
            total = (part[:, n * HALF : (n + 1) * HALF] + sides).astype(BF16)
            result[w, :, :, n * HALF : (n + 1) * HALF] = total.reshape(CHUNKS, WSTEPS, HALF)
        store(w).start()

    @pl.loop(0, WINDOWS + LAG_0)
    def _(i):
        @pl.when(i < WINDOWS)
        def _():
            make_gated(i)

        for piece, at, blocks in ((0, LAG_2, (2,)), (2, LAG_1, ()), (3, LAG_0, (0,))):

            @pl.when(i == at)
            def _():
                have_weight(piece)
                for block in blocks:
                    have_near_weight(block)

        @pl.when(i == 1)
        def _():
            @pl.loop(0, TILES)
            def _(tile):
                convolve(tile, ((0, tile),), query, EARLY, STEPS // 8)

        @pl.when((i >= LAG_2) & (i < WINDOWS + LAG_2))
        def _():
            w = i - LAG_2
            arrived(gated.at[w, :, pl.ds(0, 2 * WIDTH)], gs_sem.at[w])
            opposite(w)

            @pl.when(w == 0)
            def _():
                have_weight(1)
                have_near_weight(1)
                have_near_weight(3)

            sides_own(w)

        @pl.when((i >= LAG_1) & (i < WINDOWS + LAG_1))
        def _():
            sides_relayed(i - LAG_1)

        @pl.when(i >= LAG_0)
        def _():
            finish(i - LAG_0)

        @pl.when((i >= LAG_F) & (i < WINDOWS + LAG_F))
        def _():
            forward(i - LAG_F).start()

        for piece, at in ((2, 2), (3, 4)):

            @pl.when(i == at)
            def _():
                pass_weight(piece)

    left(halo, HALO)
    left(totals.at[pl.ds(1, SEQ - 1)], STATE)
    for kind in (WSIB, WZ, WX):
        left(wbuf.at[0], kind)
    left(gated.at[:, :, pl.ds(0, WIDTH)], NEAR)
    left(gated.at[:, :, pl.ds(0, 2 * WIDTH)], SIB)
    left(relay_out, RELAY)
    left(side_out, SIDE)
    pltpu.make_async_copy(result, result, result_sem.at[0]).wait()


def on_device(streams, short_taps, rates, residues, out_weight):
    gains = residues * jnp.sqrt(-jnp.expm1(-2.0 * rates))
    dma = pltpu.SemaphoreType.DMA
    hbm = pl.BlockSpec(memory_space=pl.ANY)
    result = pl.pallas_call(
        kernel,
        out_shape=jax.ShapeDtypeStruct((CHUNKS, STEPS, WIDTH), BF16),
        in_specs=[hbm] * 5,
        out_specs=hbm,
        scratch_shapes=[
            pltpu.VMEM((3, TAPS, WIDTH), F32),
            pltpu.VMEM((MODES, WIDTH), F32),
            pltpu.VMEM((MODES, WIDTH), F32),
            pltpu.VMEM((3, ROWS, WIDTH), BF16),
            pltpu.VMEM((3, 16, WIDTH), BF16),
            pltpu.VMEM((2 * TILES, CHUNKS * PITCH, LANES), F32),
            pltpu.VMEM((TILES, ROWS, LANES), F32),
            pltpu.VMEM((TILES, ROWS, LANES), F32),
            pltpu.VMEM((TILES, MODES, CHUNKS, LANES), F32),
            pltpu.VMEM((TILES, MODES, CHUNKS, LANES), F32),
            pltpu.VMEM((TILES, MODES, CHUNKS, LANES), F32),
            pltpu.VMEM((MODES, WIDTH), F32),
            pltpu.VMEM((SEQ, MODES, WIDTH), F32),
            pltpu.VMEM((CHUNKS * SPITCH, LANES), F32),
            pltpu.VMEM((WINDOWS, WROWS, 4 * WIDTH), BF16),
            pltpu.VMEM((4, 4, WIDTH, WIDTH), BF16),
            pltpu.VMEM((2, WINDOWS, WROWS, HALF), BF16),
            pltpu.VMEM((2, WINDOWS, WROWS, HALF), BF16),
            pltpu.VMEM((2, WINDOWS, 2, WROWS, HALF), BF16),
            pltpu.VMEM((2, WINDOWS, 2, WROWS, HALF), BF16),
            pltpu.VMEM((WINDOWS, CHUNKS, WSTEPS, WIDTH), BF16),
            dma((3,)),
            dma((3, TILES)),
            dma((9,)),
            dma((4,)),
            dma((1,)),
            dma((SEQ,)),
            dma((4,)),
            dma((4,)),
            dma((4,)),
            dma((WINDOWS,)),
            dma((WINDOWS,)),
            dma((WINDOWS,)),
            dma((WINDOWS,)),
            dma((1,)),
        ],
        compiler_params=pltpu.CompilerParams(
            collective_id=0, has_side_effects=True, vmem_limit_bytes=60 * 1024 * 1024
        ),
        cost_estimate=pl.CostEstimate(
            flops=2 * ROWS * WIDTH * 8192, bytes_accessed=16 * 1024 * 1024, transcendentals=0
        ),
        name="mixer",
    )(streams, short_taps, rates.T, gains.T, out_weight)
    return result.reshape(ROWS, WIDTH)


def solution(mesh):
    return jax.shard_map(
        on_device,
        mesh=mesh,
        in_specs=(
            P(None, "seq", "chan"),
            P(None, None, "chan"),
            P("chan", None),
            P("chan", None),
            P("chan", None),
        ),
        out_specs=P("seq", "chan"),
        check_vma=False,
    )
```

```python
import functools

import jax
import jax.numpy as jnp
from jax import lax
from jax.experimental import pallas as pl
from jax.experimental.pallas import tpu as pltpu
from jax.sharding import PartitionSpec as P

MESH = pl.DeviceIdType.MESH
F32 = jnp.float32
BF16 = jnp.bfloat16

TAPS = 7
MODES = 16
ROWS = 2048
WIDTH = 512
LANES = 128
TILES = WIDTH // LANES
CHUNKS = 8
STEPS = ROWS // CHUNKS
WINDOWS = 16
WSTEPS = STEPS // WINDOWS
WROWS = ROWS // WINDOWS
HALF = WIDTH // 2
UNROLL = 16
EARLY = 8
PAD = 8
PITCH = STEPS + PAD
SPITCH = WSTEPS + PAD
PIECES = (((2, None),), ((1, 1), (3, 0)), ((1, 0), (3, 1)), ((0, None),))
SEQ = 8
XPART = WIDTH // 4

LAG_F, LAG_2, LAG_1, LAG_0 = 2, 3, 7, 11


def kernel(
    streams, taps_in, rates_in, residues_in, weight, out,
    taps, rates, residues,
    sbuf, halo, nat, prod, query, state, decay, gain, total, totals, stage,
    gated, wbuf, relay_out, relay_in, side_out, side_in, result,
    small_sem, load_sem, out_sem, wown_sem, halo_sem, state_sem, wsib_sem, wz_sem, wx_sem,
    gz_sem, gs_sem, relay_sem, side_sem, result_sem,
):
    seq, chan = lax.axis_index("seq"), lax.axis_index("chan")
    x, zh = lax.div(seq, 2), lax.rem(seq, 2)
    y, zl, core = lax.div(chan, 4), lax.rem(lax.div(chan, 2), 2), lax.rem(chan, 2)
    mine = zl * 2 + core
    sib_chan = chan + 1 - 2 * core
    z_chan = chan + 2 - 4 * zl

    def chan_of(yy, zz, cc):
        return (yy * 2 + zz) * 2 + cc

    def y_off(k):
        return lax.rem(y + k, 4)

    sibling = (seq, sib_chan)
    z_near = (seq, z_chan)
    near = tuple((seq, chan_of(y, 1 - zl, c)) for c in range(2))
    zh_seq = seq + 1 - 2 * zh
    z_far = tuple((zh_seq, chan_of(y, 1 - zl, c)) for c in range(2))
    y_up = (seq, chan_of(y_off(1), zl, core))
    y_down = (seq, chan_of(y_off(3), zl, core))
    x_up = (lax.rem(seq + 2, SEQ), chan)
    x_down = (lax.rem(seq + 6, SEQ), chan)
    seq_of = lambda k: (lax.rem(seq + k, SEQ), chan)

    (HALO, WSIB, WZ, WX, NEAR, SIB, RELAY, SIDE) = range(8)

    def send(src, dst, kind, sem, device):
        return pltpu.make_async_remote_copy(
            src_ref=src, dst_ref=dst, send_sem=out_sem.at[kind], recv_sem=sem,
            device_id=device, device_id_type=MESH,
        )

    def arrived(ref, sem):
        send(ref, ref, 0, sem, sibling).wait_recv()

    def left(ref, kind):
        send(ref, ref, kind, halo_sem.at[0], sibling).wait_send()

    small = [
        pltpu.make_async_copy(a, b, small_sem.at[i])
        for i, (a, b) in enumerate(((rates_in, rates), (residues_in, residues), (taps_in, taps)))
    ]

    def load(j, tile):
        lanes = pl.ds(pl.multiple_of(tile * LANES, LANES), LANES)
        return pltpu.make_async_copy(streams.at[j, :, lanes], sbuf.at[j, :, lanes], load_sem.at[j, tile])

    def columns(block, n, zz, cc):
        first = chan_of(y_off(block), zz, cc) * WIDTH
        if n is None:
            return pl.ds(pl.multiple_of(first, WIDTH), WIDTH)
        return pl.ds(pl.multiple_of(first + n * HALF, HALF), HALF)

    def half(n):
        return slice(None) if n is None else pl.ds(n * HALF, HALF)

    def own_weight(block):
        return pltpu.make_async_copy(
            weight.at[:, columns(block, None, zl, core)], wbuf.at[block, mine], wown_sem.at[block]
        )

    barrier = pltpu.get_barrier_semaphore()
    partners = [seq_of(k) for k in range(1, SEQ)] + [sibling, *near, *z_far, y_up, y_down]
    for device in partners:
        pl.semaphore_signal(barrier, inc=1, device_id=device, device_id_type=MESH)
    for copy in small:
        copy.start()
    for tile in range(TILES):
        for j in (1, 2):
            load(j, tile).start()

    halo_copy = send(streams.at[:, pl.ds(ROWS - 16, 16)], halo, HALO, halo_sem.at[0], seq_of(1))

    pair = 2 * lax.rem(x, 2)
    far_sources = pl.ds(2 - 2 * zl, 2)

    def part_rows(part):
        return pl.ds(pl.multiple_of(part * XPART, XPART), XPART)

    def start_weight(piece):
        for block, n in PIECES[piece]:
            for link in range(2):
                chip = near if link == 1 and piece < 2 else z_far
                for c in range(2):
                    send(
                        weight.at[part_rows(pair + link), columns(block, n, 1 - zl, c)],
                        wbuf.at[block, mine, part_rows(pair + link), half(n)],
                        WZ, wz_sem.at[piece], chip[c],
                    ).start()

    def pass_weight(piece):
        arrived(wbuf.at[0, 0], wz_sem.at[piece])
        for block, n in PIECES[piece]:
            for way, device in enumerate((x_up, x_down)):
                there = wbuf.at[block, far_sources, part_rows(pair + way), half(n)]
                send(there, there, WX, wx_sem.at[piece], device).start()

    def have_weight(piece):
        arrived(wbuf.at[0, 0], wx_sem.at[piece])

    def near_weight(block):
        there = wbuf.at[block, mine]
        return send(weight.at[:, columns(block, None, zl, 1 - core)], there, WSIB, wsib_sem.at[block], sibling)

    def have_near_weight(block):
        arrived(wbuf.at[block, 0], wsib_sem.at[block])
        own_weight(block).wait()

    pl.semaphore_wait(barrier, len(partners))
    halo_copy.start()
    start_weight(0)
    for copy in small:
        copy.wait()

    def lanes_of(tile):
        return pl.ds(pl.multiple_of(tile * LANES, LANES), LANES)

    @pl.loop(0, TILES)
    def _(tile):
        rate = rates[:, lanes_of(tile)]
        slope = jnp.tanh(rate)
        scale = residues[:, lanes_of(tile)] * jnp.sqrt(2.0 * slope / (1.0 + slope))
        kept = jnp.exp(-rate)
        for m in range(MODES):
            decay[tile, m] = jnp.broadcast_to(kept[m : m + 1], (CHUNKS, LANES))
            gain[tile, m] = jnp.broadcast_to(scale[m : m + 1], (CHUNKS, LANES))

    first = jnp.where(seq > 0, 1.0, 0.0).astype(F32)

    def edge(j, tile, slot):
        nat[slot, pl.ds(0, PAD)] = halo[j, :, lanes_of(tile)].astype(F32)[16 - PAD :] * first

    def widen(j, tile, slot):
        lanes = lanes_of(tile)
        nat[slot, pl.ds(PAD, STEPS)] = sbuf[j, pl.ds(0, STEPS), lanes].astype(F32)

        @pl.loop(1, CHUNKS)
        def _(c):
            row = pl.multiple_of(c * STEPS - 16, 16)
            to = pl.multiple_of(c * PITCH, PAD)
            nat[slot, pl.ds(to, PITCH)] = sbuf[j, pl.ds(row, STEPS + 16), lanes].astype(F32)[16 - PAD :]

    def across(slot, step):
        return nat[slot, pl.ds(PAD + step, CHUNKS, stride=PITCH), :]

    def filtered(window, coefs):
        terms = [c * v for c, v in zip(coefs, window, strict=True)]
        while len(terms) > 1:
            terms = [a + b for a, b in zip(terms[::2], terms[1::2])] + ([terms[-1]] if len(terms) % 2 else [])
        return terms[0]

    def coefs_of(j, tile):
        return [
            jnp.broadcast_to(taps[j, pl.ds(i, 1), lanes_of(tile)], (CHUNKS, LANES)) for i in range(TAPS)
        ]

    def convolve(tile, pairs, target, first_group, groups):
        coefs = [coefs_of(j, tile) for j, _ in pairs]
        before = [tuple(across(slot, first_group * 8 - i) for i in range(1, TAPS)) for _, slot in pairs]

        def body(g, before):
            before = list(before)
            for u in range(8):
                step = g * 8 + u
                value = None
                for k, (_, slot) in enumerate(pairs):
                    window = (across(slot, step), *before[k])
                    part = filtered(window, coefs[k])
                    value = part if value is None else value * part
                    before[k] = window[:-1]
                target[tile, pl.ds(pl.multiple_of(step * CHUNKS, CHUNKS), CHUNKS)] = value
            return tuple(before)

        lax.fori_loop(first_group, groups, body, tuple(before))

    @pl.loop(0, TILES)
    def _(tile):
        load(1, tile).wait()
        load(2, tile).wait()
        widen(1, tile, 2 * tile)
        widen(2, tile, 2 * tile + 1)

        for slot in range(2):
            nat[2 * tile + slot, pl.ds(0, PAD)] = jnp.zeros((PAD, LANES), F32)
        convolve(tile, ((1, 2 * tile), (2, 2 * tile + 1)), prod, 0, STEPS // 8)

        @pl.when(tile == 2)
        def _():
            start_weight(1)
            for block in (2, 1, 3, 0):
                near_weight(block).start()
                own_weight(block).start()

    for tile in range(TILES):
        load(0, tile).start()
    arrived(halo, halo_sem.at[0])

    @pl.loop(0, TILES)
    def _(tile):
        edge(1, tile, 2 * tile)
        edge(2, tile, 2 * tile + 1)
        convolve(tile, ((1, 2 * tile), (2, 2 * tile + 1)), prod, 0, 1)

    def state_copy(k, tiles):
        return pltpu.make_async_remote_copy(
            src_ref=total.at[tiles], dst_ref=totals.at[k, tiles],
            send_sem=state_sem.at[0, k], recv_sem=state_sem.at[1, k],
            device_id=seq_of(k), device_id_type=MESH,
        )

    for k in range(1, SEQ):

        @pl.when(seq < k)
        def _():
            totals[k] = jnp.zeros((TILES, MODES, LANES), F32)

    sublane = lax.broadcasted_iota(jnp.int32, (CHUNKS, LANES), 0)

    @pl.loop(0, TILES)
    def _(tile):
        decays = [decay[tile, m] for m in range(MODES)]

        def body(g, states):
            states = list(states)
            for u in range(8):
                step = pl.multiple_of((g * 8 + u) * CHUNKS, CHUNKS)
                value = prod[tile, pl.ds(step, CHUNKS)]
                states = [a * s + value for a, s in zip(decays, states)]
            return tuple(states)

        zero = jnp.zeros((CHUNKS, LANES), F32)
        ends = lax.fori_loop(0, STEPS // 8, body, (zero,) * MODES)
        for m in range(MODES):
            rate = jnp.broadcast_to(rates[pl.ds(m, 1), lanes_of(tile)], (CHUNKS, LANES))
            run = ends[m]
            for shift in (1, 2, 4):
                moved = jnp.where(sublane >= shift, pltpu.roll(run, shift, 0), 0.0)
                run = run + jnp.exp(-rate * float(STEPS * shift)) * moved
            state[tile, m] = jnp.where(sublane >= 1, pltpu.roll(run, 1, 0), 0.0)
            total[tile, pl.ds(m, 1)] = run[CHUNKS - 1 :]

        for k in range(1, SEQ):

            @pl.when(seq + k < SEQ)
            def _():
                state_copy(k, pl.ds(tile, 1)).start()

        @pl.when(tile == 0)
        def _():
            pass_weight(0)


    @pl.loop(0, TILES)
    def _(tile):
        load(0, tile).wait()
        widen(0, tile, tile)
        edge(0, tile, tile)
        convolve(tile, ((0, tile),), query, 0, EARLY)

    start_weight(2)
    pass_weight(1)
    for k in range(1, SEQ):

        @pl.when(seq >= k)
        def _():
            state_copy(k, pl.ds(0, TILES)).wait_recv()

    @pl.loop(0, TILES)
    def _(tile):
        rate = rates[:, lanes_of(tile)]
        start = jnp.zeros((MODES, LANES), F32)
        for k in range(1, SEQ):
            part = jnp.exp(-rate * float(ROWS * (k - 1))) * totals[k, tile]
            start = start + jnp.where(seq >= k, part, 0.0)
        for m in range(MODES):
            spread = jnp.broadcast_to(rate[m : m + 1], (CHUNKS, LANES)) * (sublane * STEPS).astype(F32)
            state[tile, m] = state[tile, m] + jnp.exp(-spread) * start[m : m + 1]

    start_weight(3)
    def own_lanes():
        return pl.ds(pl.multiple_of(mine * WIDTH, WIDTH), WIDTH)

    def part_of(w, source):
        return gated.at[w, :, pl.ds(pl.multiple_of(source * WIDTH, WIDTH), WIDTH)]

    def to_near(w):
        return send(part_of(w, mine), part_of(w, mine), NEAR, gz_sem.at[w], z_near)

    def to_sibling(w):
        return send(part_of(w, mine), part_of(w, mine), SIB, gs_sem.at[w], sibling)

    def forward(w):
        source = (1 - zl) * 2 + core
        arrived(part_of(w, source), gz_sem.at[w])
        return send(part_of(w, source), part_of(w, source), SIB, gs_sem.at[w], sibling)

    def make_gated(w):
        @pl.loop(0, TILES)
        def _(tile):
            decays = [decay[tile, m] for m in range(MODES)]
            weights = [gain[tile, m] for m in range(MODES)]

            def body(g, states):
                states = list(states)
                for u in range(UNROLL):
                    at = g * UNROLL + u
                    row = pl.ds(pl.multiple_of((w * WSTEPS + at) * CHUNKS, CHUNKS), CHUNKS)
                    value = prod[tile, row]
                    states = [a * s + value for a, s in zip(decays, states)]
                    mixed = filtered(states, weights)
                    stage[pl.ds(at, CHUNKS, stride=SPITCH), :] = mixed * query[tile, row]
                return tuple(states)

            states = lax.fori_loop(0, WSTEPS // UNROLL, body, tuple(state[tile, m] for m in range(MODES)))
            for m in range(MODES):
                state[tile, m] = states[m]
            lanes = pl.ds(pl.multiple_of(mine * WIDTH + tile * LANES, LANES), LANES)
            for c in range(CHUNKS):
                rows = pl.ds(c * WSTEPS, WSTEPS)
                gated[w, rows, lanes] = stage[pl.ds(c * SPITCH, WSTEPS)].astype(BF16)

        to_near(w).start()
        to_sibling(w).start()

    def dot(w, block, n):
        columns = wbuf[block, :, :, half(n)]
        return jnp.dot(gated[w], columns.reshape(4 * WIDTH, -1), preferred_element_type=F32)

    ups = (y_up, y_down)

    def side(w, way, n):
        return send(side_out.at[way, w, n], side_in.at[way, w, n], SIDE, side_sem.at[w], ups[way])

    def store(w):
        rows = pl.ds(pl.multiple_of(w * WSTEPS, WSTEPS), WSTEPS)
        return pltpu.make_async_copy(result.at[w], out.at[:, rows], result_sem.at[0])

    def opposite(w):
        part = dot(w, 2, None).astype(BF16)
        for way in range(2):
            relay_out[way, w] = part[:, way * HALF : (way + 1) * HALF]
        for way in range(2):
            send(relay_out.at[way, w], relay_in.at[way, w], RELAY, relay_sem.at[w], ups[way]).start()

    def sides_own(w):
        parts = [dot(w, block, 1 - way).astype(BF16) for way, block in ((0, 1), (1, 3))]
        for way in range(2):
            side_out[way, w, 1 - way] = parts[way]
        for way in range(2):
            side(w, way, 1 - way).start()

    def sides_relayed(w):
        parts = [dot(w, block, way) for way, block in ((0, 1), (1, 3))]
        arrived(relay_in.at[:, w], relay_sem.at[w])
        for way in range(2):
            side_out[way, w, way] = (parts[way] + relay_in[way, w].astype(F32)).astype(BF16)
        for way in range(2):
            side(w, way, way).start()

    def finish(w):
        part = dot(w, 0, None)
        arrived(side_in.at[:, w], side_sem.at[w])
        for n in range(2):
            sides = side_in[0, w, n].astype(F32) + side_in[1, w, n].astype(F32)
            total = (part[:, n * HALF : (n + 1) * HALF] + sides).astype(BF16)
            result[w, :, :, n * HALF : (n + 1) * HALF] = total.reshape(CHUNKS, WSTEPS, HALF)
        store(w).start()

    @pl.loop(0, WINDOWS + LAG_0)
    def _(i):
        @pl.when(i < WINDOWS)
        def _():
            make_gated(i)

        for piece, at, blocks in ((0, LAG_2, (2,)), (2, LAG_1, ()), (3, LAG_0, (0,))):

            @pl.when(i == at)
            def _():
                have_weight(piece)
                for block in blocks:
                    have_near_weight(block)

        @pl.when(i == 1)
        def _():
            @pl.loop(0, TILES)
            def _(tile):
                convolve(tile, ((0, tile),), query, EARLY, STEPS // 8)

        @pl.when((i >= LAG_2) & (i < WINDOWS + LAG_2))
        def _():
            w = i - LAG_2
            arrived(gated.at[w, :, pl.ds(0, 2 * WIDTH)], gs_sem.at[w])
            opposite(w)

            @pl.when(w == 0)
            def _():
                have_weight(1)
                have_near_weight(1)
                have_near_weight(3)

            sides_own(w)

        @pl.when((i >= LAG_1) & (i < WINDOWS + LAG_1))
        def _():
            sides_relayed(i - LAG_1)

        @pl.when(i >= LAG_0)
        def _():
            finish(i - LAG_0)

        @pl.when((i >= LAG_F) & (i < WINDOWS + LAG_F))
        def _():
            forward(i - LAG_F).start()

        for piece, at in ((2, 4), (3, 8)):

            @pl.when(i == at)
            def _():
                pass_weight(piece)

    left(halo, HALO)
    for k in range(1, SEQ):

        @pl.when(seq + k < SEQ)
        def _():
            state_copy(k, pl.ds(0, TILES)).wait_send()

    for kind in (WSIB, WZ, WX):
        left(wbuf.at[0], kind)
    left(gated.at[:, :, pl.ds(0, WIDTH)], NEAR)
    left(gated.at[:, :, pl.ds(0, 2 * WIDTH)], SIB)
    left(relay_out, RELAY)
    left(side_out, SIDE)
    pltpu.make_async_copy(result, result, result_sem.at[0]).wait()


def on_device(streams, short_taps, rates, residues, out_weight):
    dma = pltpu.SemaphoreType.DMA
    hbm = pl.BlockSpec(memory_space=pl.ANY)
    result = pl.pallas_call(
        kernel,
        out_shape=jax.ShapeDtypeStruct((CHUNKS, STEPS, WIDTH), BF16),
        in_specs=[hbm] * 5,
        out_specs=hbm,
        scratch_shapes=[
            pltpu.VMEM((3, TAPS, WIDTH), F32),
            pltpu.VMEM((MODES, WIDTH), F32),
            pltpu.VMEM((MODES, WIDTH), F32),
            pltpu.VMEM((3, ROWS, WIDTH), BF16),
            pltpu.VMEM((3, 16, WIDTH), BF16),
            pltpu.VMEM((2 * TILES, CHUNKS * PITCH, LANES), F32),
            pltpu.VMEM((TILES, ROWS, LANES), F32),
            pltpu.VMEM((TILES, ROWS, LANES), F32),
            pltpu.VMEM((TILES, MODES, CHUNKS, LANES), F32),
            pltpu.VMEM((TILES, MODES, CHUNKS, LANES), F32),
            pltpu.VMEM((TILES, MODES, CHUNKS, LANES), F32),
            pltpu.VMEM((TILES, MODES, LANES), F32),
            pltpu.VMEM((SEQ, TILES, MODES, LANES), F32),
            pltpu.VMEM((CHUNKS * SPITCH, LANES), F32),
            pltpu.VMEM((WINDOWS, WROWS, 4 * WIDTH), BF16),
            pltpu.VMEM((4, 4, WIDTH, WIDTH), BF16),
            pltpu.VMEM((2, WINDOWS, WROWS, HALF), BF16),
            pltpu.VMEM((2, WINDOWS, WROWS, HALF), BF16),
            pltpu.VMEM((2, WINDOWS, 2, WROWS, HALF), BF16),
            pltpu.VMEM((2, WINDOWS, 2, WROWS, HALF), BF16),
            pltpu.VMEM((WINDOWS, CHUNKS, WSTEPS, WIDTH), BF16),
            dma((3,)),
            dma((3, TILES)),
            dma((8,)),
            dma((4,)),
            dma((1,)),
            dma((2, SEQ)),
            dma((4,)),
            dma((4,)),
            dma((4,)),
            dma((WINDOWS,)),
            dma((WINDOWS,)),
            dma((WINDOWS,)),
            dma((WINDOWS,)),
            dma((1,)),
        ],
        compiler_params=pltpu.CompilerParams(
            collective_id=0, has_side_effects=True, vmem_limit_bytes=60 * 1024 * 1024
        ),
        cost_estimate=pl.CostEstimate(
            flops=2 * ROWS * WIDTH * 8192, bytes_accessed=16 * 1024 * 1024, transcendentals=0
        ),
        name="mixer",
    )(streams, short_taps, rates.T, residues.T, out_weight)
    return result.reshape(ROWS, WIDTH)


def solution(mesh):
    return jax.shard_map(
        on_device,
        mesh=mesh,
        in_specs=(
            P(None, "seq", "chan"),
            P(None, None, "chan"),
            P("chan", None),
            P("chan", None),
            P("chan", None),
        ),
        out_specs=P("seq", "chan"),
        check_vma=False,
    )
```

```python
import functools

import jax
import jax.numpy as jnp
from jax import lax
from jax.experimental import pallas as pl
from jax.experimental.pallas import tpu as pltpu
from jax.sharding import PartitionSpec as P

MESH = pl.DeviceIdType.MESH
F32 = jnp.float32
BF16 = jnp.bfloat16

TAPS = 7
MODES = 16
ROWS = 2048
WIDTH = 512
LANES = 128
TILES = WIDTH // LANES
CHUNKS = 8
STEPS = ROWS // CHUNKS
WINDOWS = 16
WSTEPS = STEPS // WINDOWS
WROWS = ROWS // WINDOWS
HALF = WIDTH // 2
UNROLL = 16
SPAN = 512
EARLY = 4
PAD = 8
PITCH = STEPS + PAD
SPITCH = WSTEPS + PAD
PIECES = (((2, None),), ((1, 1), (3, 0)), ((1, 0), (3, 1)), ((0, None),))
SEQ = 8
XPART = WIDTH // 4

LAG_F, LAG_2, LAG_1, LAG_0 = 2, 3, 9, 13


def kernel(
    streams, taps_in, rates_in, residues_in, weight, out,
    taps, rates, residues,
    sbuf, halo, nat, prod, query, state, decay, gain, total, totals, stage,
    gated, wbuf, relay_out, relay_in, side_out, side_in, result,
    small_sem, load_sem, out_sem, wown_sem, halo_sem, state_sem, wsib_sem, wz_sem, wx_sem,
    gz_sem, gs_sem, relay_sem, side_sem, result_sem,
):
    seq, chan = lax.axis_index("seq"), lax.axis_index("chan")
    x, zh = lax.div(seq, 2), lax.rem(seq, 2)
    y, zl, core = lax.div(chan, 4), lax.rem(lax.div(chan, 2), 2), lax.rem(chan, 2)
    mine = zl * 2 + core
    sib_chan = chan + 1 - 2 * core
    z_chan = chan + 2 - 4 * zl

    def chan_of(yy, zz, cc):
        return (yy * 2 + zz) * 2 + cc

    def y_off(k):
        return lax.rem(y + k, 4)

    sibling = (seq, sib_chan)
    z_near = (seq, z_chan)
    near = tuple((seq, chan_of(y, 1 - zl, c)) for c in range(2))
    zh_seq = seq + 1 - 2 * zh
    z_far = tuple((zh_seq, chan_of(y, 1 - zl, c)) for c in range(2))
    y_up = (seq, chan_of(y_off(1), zl, core))
    y_down = (seq, chan_of(y_off(3), zl, core))
    x_up = (lax.rem(seq + 2, SEQ), chan)
    x_down = (lax.rem(seq + 6, SEQ), chan)
    seq_of = lambda k: (lax.rem(seq + k, SEQ), chan)

    (HALO, WSIB, WZ, WX, NEAR, SIB, RELAY, SIDE) = range(8)

    def send(src, dst, kind, sem, device):
        return pltpu.make_async_remote_copy(
            src_ref=src, dst_ref=dst, send_sem=out_sem.at[kind], recv_sem=sem,
            device_id=device, device_id_type=MESH,
        )

    def arrived(ref, sem):
        send(ref, ref, 0, sem, sibling).wait_recv()

    def left(ref, kind):
        send(ref, ref, kind, halo_sem.at[0], sibling).wait_send()

    small = [
        pltpu.make_async_copy(a, b, small_sem.at[i])
        for i, (a, b) in enumerate(((rates_in, rates), (residues_in, residues), (taps_in, taps)))
    ]

    def load(j, tile):
        lanes = pl.ds(pl.multiple_of(tile * LANES, LANES), LANES)
        return pltpu.make_async_copy(streams.at[j, :, lanes], sbuf.at[j, :, lanes], load_sem.at[j, tile])

    def columns(block, n, zz, cc):
        first = chan_of(y_off(block), zz, cc) * WIDTH
        if n is None:
            return pl.ds(pl.multiple_of(first, WIDTH), WIDTH)
        return pl.ds(pl.multiple_of(first + n * HALF, HALF), HALF)

    def half(n):
        return slice(None) if n is None else pl.ds(n * HALF, HALF)

    def own_weight(block):
        return pltpu.make_async_copy(
            weight.at[:, columns(block, None, zl, core)], wbuf.at[block, mine], wown_sem.at[block]
        )

    barrier = pltpu.get_barrier_semaphore()
    partners = [seq_of(k) for k in range(1, SEQ)] + [sibling, *near, *z_far, y_up, y_down]
    for device in partners:
        pl.semaphore_signal(barrier, inc=1, device_id=device, device_id_type=MESH)
    for copy in small:
        copy.start()
    for tile in range(TILES):
        for j in (1, 2):
            load(j, tile).start()

    halo_copy = send(streams.at[:, pl.ds(ROWS - 16, 16)], halo, HALO, halo_sem.at[0], seq_of(1))

    pair = 2 * lax.rem(x, 2)
    far_sources = pl.ds(2 - 2 * zl, 2)

    def part_rows(part):
        return pl.ds(pl.multiple_of(part * XPART, XPART), XPART)

    def start_weight(piece):
        for block, n in PIECES[piece]:
            for link in range(2):
                chip = near if link == 1 and piece < 2 else z_far
                for c in range(2):
                    send(
                        weight.at[part_rows(pair + link), columns(block, n, 1 - zl, c)],
                        wbuf.at[block, mine, part_rows(pair + link), half(n)],
                        WZ, wz_sem.at[piece], chip[c],
                    ).start()

    def pass_weight(piece):
        arrived(wbuf.at[0, 0], wz_sem.at[piece])
        for block, n in PIECES[piece]:
            for way, device in enumerate((x_up, x_down)):
                there = wbuf.at[block, far_sources, part_rows(pair + way), half(n)]
                send(there, there, WX, wx_sem.at[piece], device).start()

    def have_weight(piece):
        arrived(wbuf.at[0, 0], wx_sem.at[piece])

    def near_weight(block):
        there = wbuf.at[block, mine]
        return send(weight.at[:, columns(block, None, zl, 1 - core)], there, WSIB, wsib_sem.at[block], sibling)

    def have_near_weight(block):
        arrived(wbuf.at[block, 0], wsib_sem.at[block])
        own_weight(block).wait()

    pl.semaphore_wait(barrier, len(partners))
    halo_copy.start()
    start_weight(0)
    for copy in small:
        copy.wait()

    def lanes_of(tile):
        return pl.ds(pl.multiple_of(tile * LANES, LANES), LANES)

    @pl.loop(0, TILES)
    def _(tile):
        rate = rates[:, lanes_of(tile)]
        slope = jnp.tanh(rate)
        scale = residues[:, lanes_of(tile)] * jnp.sqrt(2.0 * slope / (1.0 + slope))
        kept = jnp.exp(-rate)
        for m in range(MODES):
            decay[tile, m] = jnp.broadcast_to(kept[m : m + 1], (CHUNKS, LANES))
            gain[tile, m] = jnp.broadcast_to(scale[m : m + 1], (CHUNKS, LANES))

    first = jnp.where(seq > 0, 1.0, 0.0).astype(F32)

    def edge(j, tile, slot):
        nat[slot, pl.ds(0, PAD)] = halo[j, :, lanes_of(tile)].astype(F32)[16 - PAD :] * first

    def widen(j, tile, slot):
        lanes = lanes_of(tile)
        nat[slot, pl.ds(PAD, STEPS)] = sbuf[j, pl.ds(0, STEPS), lanes].astype(F32)

        @pl.loop(1, CHUNKS)
        def _(c):
            row = pl.multiple_of(c * STEPS - 16, 16)
            to = pl.multiple_of(c * PITCH, PAD)
            nat[slot, pl.ds(to, PITCH)] = sbuf[j, pl.ds(row, STEPS + 16), lanes].astype(F32)[16 - PAD :]

    def across(slot, step):
        return nat[slot, pl.ds(PAD + step, CHUNKS, stride=PITCH), :]

    def filtered(window, coefs):
        terms = [c * v for c, v in zip(coefs, window, strict=True)]
        while len(terms) > 1:
            terms = [a + b for a, b in zip(terms[::2], terms[1::2])] + ([terms[-1]] if len(terms) % 2 else [])
        return terms[0]

    def coefs_of(j, tile):
        return [
            jnp.broadcast_to(taps[j, pl.ds(i, 1), lanes_of(tile)], (CHUNKS, LANES)) for i in range(TAPS)
        ]

    def convolve(tile, pairs, target, first_group, groups):
        coefs = [coefs_of(j, tile) for j, _ in pairs]
        before = [tuple(across(slot, first_group * UNROLL - i) for i in range(1, TAPS)) for _, slot in pairs]

        def body(g, before):
            before = list(before)
            for u in range(UNROLL):
                step = g * UNROLL + u
                value = None
                for k, (_, slot) in enumerate(pairs):
                    window = (across(slot, step), *before[k])
                    part = filtered(window, coefs[k])
                    value = part if value is None else value * part
                    before[k] = window[:-1]
                target[tile, pl.ds(pl.multiple_of(step * CHUNKS, CHUNKS), CHUNKS)] = value
            return tuple(before)

        lax.fori_loop(first_group, groups, body, tuple(before))

    @pl.loop(0, TILES)
    def _(tile):
        load(1, tile).wait()
        load(2, tile).wait()
        widen(1, tile, 2 * tile)
        widen(2, tile, 2 * tile + 1)

        for slot in range(2):
            nat[2 * tile + slot, pl.ds(0, PAD)] = jnp.zeros((PAD, LANES), F32)
        convolve(tile, ((1, 2 * tile), (2, 2 * tile + 1)), prod, 0, STEPS // UNROLL)

        @pl.when(tile == 2)
        def _():
            start_weight(1)
            for block in (2, 1, 3, 0):
                near_weight(block).start()
                own_weight(block).start()

    for tile in range(TILES):
        load(0, tile).start()
    arrived(halo, halo_sem.at[0])

    @pl.loop(0, TILES)
    def _(tile):
        edge(1, tile, 2 * tile)
        edge(2, tile, 2 * tile + 1)
        convolve(tile, ((1, 2 * tile), (2, 2 * tile + 1)), prod, 0, 1)

    def state_copy(k, tiles):
        return pltpu.make_async_remote_copy(
            src_ref=total.at[tiles], dst_ref=totals.at[k, tiles],
            send_sem=state_sem.at[0, k], recv_sem=state_sem.at[1, k],
            device_id=seq_of(k), device_id_type=MESH,
        )

    for k in range(1, SEQ):

        @pl.when(seq < k)
        def _():
            totals[k] = jnp.zeros((TILES, MODES, LANES), F32)

    sublane = lax.broadcasted_iota(jnp.int32, (CHUNKS, LANES), 0)

    @pl.loop(0, TILES)
    def _(tile):
        decays = [decay[tile, m] for m in range(MODES)]

        def body(g, states):
            states = list(states)
            for u in range(UNROLL):
                step = pl.multiple_of((g * UNROLL + u) * CHUNKS, CHUNKS)
                value = prod[tile, pl.ds(step, CHUNKS)]
                states = [a * s + value for a, s in zip(decays, states)]
            return tuple(states)

        zero = jnp.zeros((CHUNKS, LANES), F32)
        ends = lax.fori_loop(0, STEPS // UNROLL, body, (zero,) * MODES)
        for m in range(MODES):
            rate = jnp.broadcast_to(rates[pl.ds(m, 1), lanes_of(tile)], (CHUNKS, LANES))
            run = ends[m]
            for shift in (1, 2, 4):
                moved = jnp.where(sublane >= shift, pltpu.roll(run, shift, 0), 0.0)
                run = run + jnp.exp(-rate * float(STEPS * shift)) * moved
            state[tile, m] = jnp.where(sublane >= 1, pltpu.roll(run, 1, 0), 0.0)
            total[tile, pl.ds(m, 1)] = run[CHUNKS - 1 :]

        for k in range(1, SEQ):

            @pl.when(seq + k < SEQ)
            def _():
                state_copy(k, pl.ds(tile, 1)).start()

        @pl.when(tile == 0)
        def _():
            pass_weight(0)


    @pl.loop(0, TILES)
    def _(tile):
        load(0, tile).wait()
        widen(0, tile, tile)
        edge(0, tile, tile)
        convolve(tile, ((0, tile),), query, 0, EARLY)

    start_weight(2)
    pass_weight(1)
    for k in range(1, SEQ):

        @pl.when(seq >= k)
        def _():
            state_copy(k, pl.ds(0, TILES)).wait_recv()

    @pl.loop(0, TILES)
    def _(tile):
        rate = rates[:, lanes_of(tile)]
        start = jnp.zeros((MODES, LANES), F32)
        for k in range(1, SEQ):
            part = jnp.exp(-rate * float(ROWS * (k - 1))) * totals[k, tile]
            start = start + jnp.where(seq >= k, part, 0.0)
        for m in range(MODES):
            spread = jnp.broadcast_to(rate[m : m + 1], (CHUNKS, LANES)) * (sublane * STEPS).astype(F32)
            state[tile, m] = state[tile, m] + jnp.exp(-spread) * start[m : m + 1]

    start_weight(3)
    def own_lanes():
        return pl.ds(pl.multiple_of(mine * WIDTH, WIDTH), WIDTH)

    def part_of(w, source):
        return gated.at[w, :, pl.ds(pl.multiple_of(source * WIDTH, WIDTH), WIDTH)]

    def to_near(w):
        return send(part_of(w, mine), part_of(w, mine), NEAR, gz_sem.at[w], z_near)

    def to_sibling(w):
        return send(part_of(w, mine), part_of(w, mine), SIB, gs_sem.at[w], sibling)

    def forward(w):
        source = (1 - zl) * 2 + core
        arrived(part_of(w, source), gz_sem.at[w])
        return send(part_of(w, source), part_of(w, source), SIB, gs_sem.at[w], sibling)

    def make_gated(w):
        @pl.loop(0, TILES)
        def _(tile):
            decays = [decay[tile, m] for m in range(MODES)]
            weights = [gain[tile, m] for m in range(MODES)]

            def body(g, states):
                states = list(states)
                for u in range(UNROLL):
                    at = g * UNROLL + u
                    row = pl.ds(pl.multiple_of((w * WSTEPS + at) * CHUNKS, CHUNKS), CHUNKS)
                    value = prod[tile, row]
                    states = [a * s + value for a, s in zip(decays, states)]
                    mixed = filtered(states, weights)
                    stage[pl.ds(at, CHUNKS, stride=SPITCH), :] = mixed * query[tile, row]
                return tuple(states)

            states = lax.fori_loop(0, WSTEPS // UNROLL, body, tuple(state[tile, m] for m in range(MODES)))
            for m in range(MODES):
                state[tile, m] = states[m]
            lanes = pl.ds(pl.multiple_of(mine * WIDTH + tile * LANES, LANES), LANES)
            for c in range(CHUNKS):
                rows = pl.ds(c * WSTEPS, WSTEPS)
                gated[w, rows, lanes] = stage[pl.ds(c * SPITCH, WSTEPS)].astype(BF16)

        to_near(w).start()
        to_sibling(w).start()

    def dot(w, block, n):
        columns = wbuf[block, :, :, half(n)]
        return jnp.dot(gated[w], columns.reshape(4 * WIDTH, -1), preferred_element_type=F32)

    ups = (y_up, y_down)

    def side(w, way, n):
        return send(side_out.at[way, w, n], side_in.at[way, w, n], SIDE, side_sem.at[w], ups[way])

    def store(w):
        rows = pl.ds(pl.multiple_of(w * WSTEPS, WSTEPS), WSTEPS)
        return pltpu.make_async_copy(result.at[w], out.at[:, rows], result_sem.at[0])

    def opposite(w):
        part = dot(w, 2, None).astype(BF16)
        for way in range(2):
            relay_out[way, w] = part[:, way * HALF : (way + 1) * HALF]
        for way in range(2):
            send(relay_out.at[way, w], relay_in.at[way, w], RELAY, relay_sem.at[w], ups[way]).start()

    def sides_own(w):
        parts = [dot(w, block, 1 - way).astype(BF16) for way, block in ((0, 1), (1, 3))]
        for way in range(2):
            side_out[way, w, 1 - way] = parts[way]
        for way in range(2):
            side(w, way, 1 - way).start()

    def sides_relayed(w):
        parts = [dot(w, block, way) for way, block in ((0, 1), (1, 3))]
        arrived(relay_in.at[:, w], relay_sem.at[w])
        for way in range(2):
            side_out[way, w, way] = (parts[way] + relay_in[way, w].astype(F32)).astype(BF16)
        for way in range(2):
            side(w, way, way).start()

    def finish(w):
        part = dot(w, 0, None)
        arrived(side_in.at[:, w], side_sem.at[w])
        for n in range(2):
            sides = side_in[0, w, n].astype(F32) + side_in[1, w, n].astype(F32)
            total = (part[:, n * HALF : (n + 1) * HALF] + sides).astype(BF16)
            result[w, :, :, n * HALF : (n + 1) * HALF] = total.reshape(CHUNKS, WSTEPS, HALF)
        store(w).start()

    @pl.loop(0, WINDOWS + LAG_0)
    def _(i):
        @pl.when(i < WINDOWS)
        def _():
            make_gated(i)

        for piece, at, blocks in ((0, LAG_2, (2,)), (2, LAG_1, ()), (3, LAG_0, (0,))):

            @pl.when(i == at)
            def _():
                have_weight(piece)
                for block in blocks:
                    have_near_weight(block)

        @pl.when(i == 1)
        def _():
            @pl.loop(0, TILES)
            def _(tile):
                convolve(tile, ((0, tile),), query, EARLY, STEPS // UNROLL)

        @pl.when((i >= LAG_2) & (i < WINDOWS + LAG_2))
        def _():
            w = i - LAG_2
            arrived(gated.at[w, :, pl.ds(0, 2 * WIDTH)], gs_sem.at[w])
            opposite(w)

            @pl.when(w == 0)
            def _():
                have_weight(1)
                have_near_weight(1)
                have_near_weight(3)

            sides_own(w)

        @pl.when((i >= LAG_1) & (i < WINDOWS + LAG_1))
        def _():
            sides_relayed(i - LAG_1)

        @pl.when(i >= LAG_0)
        def _():
            finish(i - LAG_0)

        @pl.when((i >= LAG_F) & (i < WINDOWS + LAG_F))
        def _():
            forward(i - LAG_F).start()

        for piece, at in ((2, 5), (3, 9)):

            @pl.when(i == at)
            def _():
                pass_weight(piece)

    left(halo, HALO)
    for k in range(1, SEQ):

        @pl.when(seq + k < SEQ)
        def _():
            state_copy(k, pl.ds(0, TILES)).wait_send()

    for kind in (WSIB, WZ, WX):
        left(wbuf.at[0], kind)
    left(gated.at[:, :, pl.ds(0, WIDTH)], NEAR)
    left(gated.at[:, :, pl.ds(0, 2 * WIDTH)], SIB)
    left(relay_out, RELAY)
    left(side_out, SIDE)
    pltpu.make_async_copy(result, result, result_sem.at[0]).wait()


def hand_on(source, target, buffer, sems):
    def part(i, into):
        rows = pl.ds(i * SPAN, SPAN)
        if into:
            return pltpu.make_async_copy(source.at[rows], buffer.at[rows], sems.at[0, i])
        return pltpu.make_async_copy(buffer.at[rows], target.at[rows], sems.at[1, i])

    for i in range(ROWS // SPAN):
        part(i, True).start()
    for i in range(ROWS // SPAN):
        part(i, True).wait()
        part(i, False).start()
    for i in range(ROWS // SPAN):
        part(i, False).wait()


def on_device(streams, short_taps, rates, residues, out_weight):
    dma = pltpu.SemaphoreType.DMA
    hbm = pl.BlockSpec(memory_space=pl.ANY)
    result = pl.pallas_call(
        kernel,
        out_shape=jax.ShapeDtypeStruct((CHUNKS, STEPS, WIDTH), BF16),
        in_specs=[hbm] * 5,
        out_specs=hbm,
        scratch_shapes=[
            pltpu.VMEM((3, TAPS, WIDTH), F32),
            pltpu.VMEM((MODES, WIDTH), F32),
            pltpu.VMEM((MODES, WIDTH), F32),
            pltpu.VMEM((3, ROWS, WIDTH), BF16),
            pltpu.VMEM((3, 16, WIDTH), BF16),
            pltpu.VMEM((2 * TILES, CHUNKS * PITCH, LANES), F32),
            pltpu.VMEM((TILES, ROWS, LANES), F32),
            pltpu.VMEM((TILES, ROWS, LANES), F32),
            pltpu.VMEM((TILES, MODES, CHUNKS, LANES), F32),
            pltpu.VMEM((TILES, MODES, CHUNKS, LANES), F32),
            pltpu.VMEM((TILES, MODES, CHUNKS, LANES), F32),
            pltpu.VMEM((TILES, MODES, LANES), F32),
            pltpu.VMEM((SEQ, TILES, MODES, LANES), F32),
            pltpu.VMEM((CHUNKS * SPITCH, LANES), F32),
            pltpu.VMEM((WINDOWS, WROWS, 4 * WIDTH), BF16),
            pltpu.VMEM((4, 4, WIDTH, WIDTH), BF16),
            pltpu.VMEM((2, WINDOWS, WROWS, HALF), BF16),
            pltpu.VMEM((2, WINDOWS, WROWS, HALF), BF16),
            pltpu.VMEM((2, WINDOWS, 2, WROWS, HALF), BF16),
            pltpu.VMEM((2, WINDOWS, 2, WROWS, HALF), BF16),
            pltpu.VMEM((WINDOWS, CHUNKS, WSTEPS, WIDTH), BF16),
            dma((3,)),
            dma((3, TILES)),
            dma((8,)),
            dma((4,)),
            dma((1,)),
            dma((2, SEQ)),
            dma((4,)),
            dma((4,)),
            dma((4,)),
            dma((WINDOWS,)),
            dma((WINDOWS,)),
            dma((WINDOWS,)),
            dma((WINDOWS,)),
            dma((1,)),
        ],
        compiler_params=pltpu.CompilerParams(
            collective_id=0, has_side_effects=True, vmem_limit_bytes=60 * 1024 * 1024
        ),
        cost_estimate=pl.CostEstimate(
            flops=2 * ROWS * WIDTH * 8192, bytes_accessed=16 * 1024 * 1024, transcendentals=0
        ),
        name="mixer",
    )(streams, short_taps, rates.T, residues.T, out_weight)
    return pl.pallas_call(
        hand_on,
        out_shape=jax.ShapeDtypeStruct((ROWS, WIDTH), BF16),
        in_specs=[hbm],
        out_specs=hbm,
        scratch_shapes=[pltpu.VMEM((ROWS, WIDTH), BF16), dma((2, ROWS // SPAN))],
        cost_estimate=pl.CostEstimate(flops=0, bytes_accessed=4 * ROWS * WIDTH, transcendentals=0),
        name="hand_on",
    )(result.reshape(ROWS, WIDTH))


def solution(mesh):
    return jax.shard_map(
        on_device,
        mesh=mesh,
        in_specs=(
            P(None, "seq", "chan"),
            P(None, None, "chan"),
            P("chan", None),
            P("chan", None),
            P("chan", None),
        ),
        out_specs=P("seq", "chan"),
        check_vma=False,
    )
```

```python
import functools

import jax
import jax.numpy as jnp
from jax import lax
from jax.experimental import pallas as pl
from jax.experimental.pallas import tpu as pltpu
from jax.sharding import PartitionSpec as P

MESH = pl.DeviceIdType.MESH
F32 = jnp.float32
BF16 = jnp.bfloat16

TAPS = 7
MODES = 16
ROWS = 2048
WIDTH = 512
LANES = 128
TILES = WIDTH // LANES
CHUNKS = 8
STEPS = ROWS // CHUNKS
WINDOWS = 16
WSTEPS = STEPS // WINDOWS
WROWS = ROWS // WINDOWS
HALF = WIDTH // 2
UNROLL = 16
SPAN = 512
EARLY = 4
PAD = 8
PITCH = STEPS + PAD
SPITCH = WSTEPS + PAD
PIECES = (((2, 0),), ((2, 1),), ((1, 1), (3, 0)), ((1, 0), (3, 1)), ((0, None),))
SEQ = 8
XPART = WIDTH // 4

LAG_F, LAG_2, LAG_1, LAG_0 = 2, 3, 9, 13


def kernel(
    streams, taps_in, rates_in, residues_in, weight, out,
    taps, rates, residues,
    sbuf, halo, nat, prod, query, state, decay, gain, total, totals, stage,
    gated, wbuf, relay_out, relay_in, side_out, side_in, result,
    small_sem, load_sem, out_sem, wown_sem, halo_sem, state_sem, wsib_sem, wz_sem, wx_sem,
    gz_sem, gs_sem, relay_sem, side_sem, result_sem,
):
    seq, chan = lax.axis_index("seq"), lax.axis_index("chan")
    x, zh = lax.div(seq, 2), lax.rem(seq, 2)
    y, zl, core = lax.div(chan, 4), lax.rem(lax.div(chan, 2), 2), lax.rem(chan, 2)
    mine = zl * 2 + core
    sib_chan = chan + 1 - 2 * core
    z_chan = chan + 2 - 4 * zl

    def chan_of(yy, zz, cc):
        return (yy * 2 + zz) * 2 + cc

    def y_off(k):
        return lax.rem(y + k, 4)

    sibling = (seq, sib_chan)
    z_near = (seq, z_chan)
    near = tuple((seq, chan_of(y, 1 - zl, c)) for c in range(2))
    zh_seq = seq + 1 - 2 * zh
    z_far = tuple((zh_seq, chan_of(y, 1 - zl, c)) for c in range(2))
    y_up = (seq, chan_of(y_off(1), zl, core))
    y_down = (seq, chan_of(y_off(3), zl, core))
    x_up = (lax.rem(seq + 2, SEQ), chan)
    x_down = (lax.rem(seq + 6, SEQ), chan)
    seq_of = lambda k: (lax.rem(seq + k, SEQ), chan)

    (HALO, WSIB, WZ, WX, NEAR, SIB, RELAY, SIDE) = range(8)

    def send(src, dst, kind, sem, device):
        return pltpu.make_async_remote_copy(
            src_ref=src, dst_ref=dst, send_sem=out_sem.at[kind], recv_sem=sem,
            device_id=device, device_id_type=MESH,
        )

    def arrived(ref, sem):
        send(ref, ref, 0, sem, sibling).wait_recv()

    def left(ref, kind):
        send(ref, ref, kind, halo_sem.at[0], sibling).wait_send()

    small = [
        pltpu.make_async_copy(a, b, small_sem.at[i])
        for i, (a, b) in enumerate(((rates_in, rates), (residues_in, residues), (taps_in, taps)))
    ]

    def load(j, tile):
        lanes = pl.ds(pl.multiple_of(tile * LANES, LANES), LANES)
        return pltpu.make_async_copy(streams.at[j, :, lanes], sbuf.at[j, :, lanes], load_sem.at[j, tile])

    def columns(block, n, zz, cc):
        first = chan_of(y_off(block), zz, cc) * WIDTH
        if n is None:
            return pl.ds(pl.multiple_of(first, WIDTH), WIDTH)
        return pl.ds(pl.multiple_of(first + n * HALF, HALF), HALF)

    def half(n):
        return slice(None) if n is None else pl.ds(n * HALF, HALF)

    def own_weight(block):
        return pltpu.make_async_copy(
            weight.at[:, columns(block, None, zl, core)], wbuf.at[block, mine], wown_sem.at[block]
        )

    barrier = pltpu.get_barrier_semaphore()
    partners = [seq_of(k) for k in range(1, SEQ)] + [sibling, *near, *z_far, y_up, y_down]
    for device in partners:
        pl.semaphore_signal(barrier, inc=1, device_id=device, device_id_type=MESH)
    for copy in small:
        copy.start()
    for tile in range(TILES):
        for j in (1, 2):
            load(j, tile).start()

    halo_copy = send(streams.at[:, pl.ds(ROWS - 16, 16)], halo, HALO, halo_sem.at[0], seq_of(1))

    pair = 2 * lax.rem(x, 2)
    far_sources = pl.ds(2 - 2 * zl, 2)

    def part_rows(part):
        return pl.ds(pl.multiple_of(part * XPART, XPART), XPART)

    def piece_rows(piece):
        return HALF if piece < 2 else WIDTH

    def start_weight(piece):
        for block, n in PIECES[piece]:
            for link in range(2):
                chip = near if link == 1 and piece < 3 else z_far
                for c in range(2):
                    send(
                        weight.at[part_rows(pair + link), columns(block, n, 1 - zl, c)],
                        wbuf.at[block, mine, part_rows(pair + link), half(n)],
                        WZ, wz_sem.at[piece], chip[c],
                    ).start()

    def pass_weight(piece):
        arrived(wbuf.at[0, 0, pl.ds(0, piece_rows(piece))], wz_sem.at[piece])
        for block, n in PIECES[piece]:
            for way, device in enumerate((x_up, x_down)):
                there = wbuf.at[block, far_sources, part_rows(pair + way), half(n)]
                send(there, there, WX, wx_sem.at[piece], device).start()

    def have_weight(piece):
        arrived(wbuf.at[0, 0, pl.ds(0, piece_rows(piece))], wx_sem.at[piece])

    def near_weight(block):
        there = wbuf.at[block, mine]
        return send(weight.at[:, columns(block, None, zl, 1 - core)], there, WSIB, wsib_sem.at[block], sibling)

    def have_near_weight(block):
        arrived(wbuf.at[block, 0], wsib_sem.at[block])
        own_weight(block).wait()

    pl.semaphore_wait(barrier, len(partners))
    halo_copy.start()
    start_weight(0)
    for copy in small:
        copy.wait()

    def lanes_of(tile):
        return pl.ds(pl.multiple_of(tile * LANES, LANES), LANES)

    @pl.loop(0, TILES)
    def _(tile):
        rate = rates[:, lanes_of(tile)]
        slope = jnp.tanh(rate)
        scale = residues[:, lanes_of(tile)] * jnp.sqrt(2.0 * slope / (1.0 + slope))
        kept = jnp.exp(-rate)
        for m in range(MODES):
            decay[tile, m] = jnp.broadcast_to(kept[m : m + 1], (CHUNKS, LANES))
            gain[tile, m] = jnp.broadcast_to(scale[m : m + 1], (CHUNKS, LANES))

    first = jnp.where(seq > 0, 1.0, 0.0).astype(F32)

    def edge(j, tile, slot):
        nat[slot, pl.ds(0, PAD)] = halo[j, :, lanes_of(tile)].astype(F32)[16 - PAD :] * first

    def widen(j, tile, slot):
        lanes = lanes_of(tile)
        nat[slot, pl.ds(PAD, STEPS)] = sbuf[j, pl.ds(0, STEPS), lanes].astype(F32)

        @pl.loop(1, CHUNKS)
        def _(c):
            row = pl.multiple_of(c * STEPS - 16, 16)
            to = pl.multiple_of(c * PITCH, PAD)
            nat[slot, pl.ds(to, PITCH)] = sbuf[j, pl.ds(row, STEPS + 16), lanes].astype(F32)[16 - PAD :]

    def across(slot, step):
        return nat[slot, pl.ds(PAD + step, CHUNKS, stride=PITCH), :]

    def filtered(window, coefs):
        terms = [c * v for c, v in zip(coefs, window, strict=True)]
        while len(terms) > 1:
            terms = [a + b for a, b in zip(terms[::2], terms[1::2])] + ([terms[-1]] if len(terms) % 2 else [])
        return terms[0]

    def coefs_of(j, tile):
        return [
            jnp.broadcast_to(taps[j, pl.ds(i, 1), lanes_of(tile)], (CHUNKS, LANES)) for i in range(TAPS)
        ]

    def convolve(tile, pairs, target, first_group, groups):
        coefs = [coefs_of(j, tile) for j, _ in pairs]
        before = [tuple(across(slot, first_group * UNROLL - i) for i in range(1, TAPS)) for _, slot in pairs]

        def body(g, before):
            before = list(before)
            for u in range(UNROLL):
                step = g * UNROLL + u
                value = None
                for k, (_, slot) in enumerate(pairs):
                    window = (across(slot, step), *before[k])
                    part = filtered(window, coefs[k])
                    value = part if value is None else value * part
                    before[k] = window[:-1]
                target[tile, pl.ds(pl.multiple_of(step * CHUNKS, CHUNKS), CHUNKS)] = value
            return tuple(before)

        lax.fori_loop(first_group, groups, body, tuple(before))

    @pl.loop(0, TILES)
    def _(tile):
        load(1, tile).wait()
        load(2, tile).wait()
        widen(1, tile, 2 * tile)
        widen(2, tile, 2 * tile + 1)

        for slot in range(2):
            nat[2 * tile + slot, pl.ds(0, PAD)] = jnp.zeros((PAD, LANES), F32)
        convolve(tile, ((1, 2 * tile), (2, 2 * tile + 1)), prod, 0, STEPS // UNROLL)

        @pl.when(tile == 0)
        def _():
            start_weight(1)

        @pl.when(tile == 2)
        def _():
            pass_weight(0)

        @pl.when(tile == 2)
        def _():
            start_weight(2)
            for block in (2, 1, 3, 0):
                near_weight(block).start()
                own_weight(block).start()

    for tile in range(TILES):
        load(0, tile).start()
    arrived(halo, halo_sem.at[0])

    @pl.loop(0, TILES)
    def _(tile):
        edge(1, tile, 2 * tile)
        edge(2, tile, 2 * tile + 1)
        convolve(tile, ((1, 2 * tile), (2, 2 * tile + 1)), prod, 0, 1)

    def state_copy(k, tiles):
        return pltpu.make_async_remote_copy(
            src_ref=total.at[tiles], dst_ref=totals.at[k, tiles],
            send_sem=state_sem.at[0, k], recv_sem=state_sem.at[1, k],
            device_id=seq_of(k), device_id_type=MESH,
        )

    for k in range(1, SEQ):

        @pl.when(seq < k)
        def _():
            totals[k] = jnp.zeros((TILES, MODES, LANES), F32)

    sublane = lax.broadcasted_iota(jnp.int32, (CHUNKS, LANES), 0)

    @pl.loop(0, TILES)
    def _(tile):
        decays = [decay[tile, m] for m in range(MODES)]

        def body(g, states):
            states = list(states)
            for u in range(UNROLL):
                step = pl.multiple_of((g * UNROLL + u) * CHUNKS, CHUNKS)
                value = prod[tile, pl.ds(step, CHUNKS)]
                states = [a * s + value for a, s in zip(decays, states)]
            return tuple(states)

        zero = jnp.zeros((CHUNKS, LANES), F32)
        ends = lax.fori_loop(0, STEPS // UNROLL, body, (zero,) * MODES)
        for m in range(MODES):
            rate = jnp.broadcast_to(rates[pl.ds(m, 1), lanes_of(tile)], (CHUNKS, LANES))
            run = ends[m]
            for shift in (1, 2, 4):
                moved = jnp.where(sublane >= shift, pltpu.roll(run, shift, 0), 0.0)
                run = run + jnp.exp(-rate * float(STEPS * shift)) * moved
            state[tile, m] = jnp.where(sublane >= 1, pltpu.roll(run, 1, 0), 0.0)
            total[tile, pl.ds(m, 1)] = run[CHUNKS - 1 :]

        for k in range(1, SEQ):

            @pl.when(seq + k < SEQ)
            def _():
                state_copy(k, pl.ds(tile, 1)).start()

        @pl.when(tile == 0)
        def _():
            pass_weight(1)


    @pl.loop(0, TILES)
    def _(tile):
        load(0, tile).wait()
        widen(0, tile, tile)
        edge(0, tile, tile)
        convolve(tile, ((0, tile),), query, 0, EARLY)

    start_weight(3)
    pass_weight(2)
    for k in range(1, SEQ):

        @pl.when(seq >= k)
        def _():
            state_copy(k, pl.ds(0, TILES)).wait_recv()

    @pl.loop(0, TILES)
    def _(tile):
        rate = rates[:, lanes_of(tile)]
        start = jnp.zeros((MODES, LANES), F32)
        for k in range(1, SEQ):
            part = jnp.exp(-rate * float(ROWS * (k - 1))) * totals[k, tile]
            start = start + jnp.where(seq >= k, part, 0.0)
        for m in range(MODES):
            spread = jnp.broadcast_to(rate[m : m + 1], (CHUNKS, LANES)) * (sublane * STEPS).astype(F32)
            state[tile, m] = state[tile, m] + jnp.exp(-spread) * start[m : m + 1]

    start_weight(4)
    def own_lanes():
        return pl.ds(pl.multiple_of(mine * WIDTH, WIDTH), WIDTH)

    def part_of(w, source):
        return gated.at[w, :, pl.ds(pl.multiple_of(source * WIDTH, WIDTH), WIDTH)]

    def to_near(w):
        return send(part_of(w, mine), part_of(w, mine), NEAR, gz_sem.at[w], z_near)

    def to_sibling(w):
        return send(part_of(w, mine), part_of(w, mine), SIB, gs_sem.at[w], sibling)

    def forward(w):
        source = (1 - zl) * 2 + core
        arrived(part_of(w, source), gz_sem.at[w])
        return send(part_of(w, source), part_of(w, source), SIB, gs_sem.at[w], sibling)

    def make_gated(w):
        @pl.loop(0, TILES)
        def _(tile):
            decays = [decay[tile, m] for m in range(MODES)]
            weights = [gain[tile, m] for m in range(MODES)]

            def body(g, states):
                states = list(states)
                for u in range(UNROLL):
                    at = g * UNROLL + u
                    row = pl.ds(pl.multiple_of((w * WSTEPS + at) * CHUNKS, CHUNKS), CHUNKS)
                    value = prod[tile, row]
                    states = [a * s + value for a, s in zip(decays, states)]
                    mixed = filtered(states, weights)
                    stage[pl.ds(at, CHUNKS, stride=SPITCH), :] = mixed * query[tile, row]
                return tuple(states)

            states = lax.fori_loop(0, WSTEPS // UNROLL, body, tuple(state[tile, m] for m in range(MODES)))
            for m in range(MODES):
                state[tile, m] = states[m]
            lanes = pl.ds(pl.multiple_of(mine * WIDTH + tile * LANES, LANES), LANES)
            for c in range(CHUNKS):
                rows = pl.ds(c * WSTEPS, WSTEPS)
                gated[w, rows, lanes] = stage[pl.ds(c * SPITCH, WSTEPS)].astype(BF16)

        to_near(w).start()
        to_sibling(w).start()

    def dot(w, block, n):
        columns = wbuf[block, :, :, half(n)]
        return jnp.dot(gated[w], columns.reshape(4 * WIDTH, -1), preferred_element_type=F32)

    ups = (y_up, y_down)

    def side(w, way, n):
        return send(side_out.at[way, w, n], side_in.at[way, w, n], SIDE, side_sem.at[w], ups[way])

    def store(w):
        rows = pl.ds(pl.multiple_of(w * WSTEPS, WSTEPS), WSTEPS)
        return pltpu.make_async_copy(result.at[w], out.at[:, rows], result_sem.at[0])

    def opposite(w):
        part = dot(w, 2, None).astype(BF16)
        for way in range(2):
            relay_out[way, w] = part[:, way * HALF : (way + 1) * HALF]
        for way in range(2):
            send(relay_out.at[way, w], relay_in.at[way, w], RELAY, relay_sem.at[w], ups[way]).start()

    def sides_own(w):
        parts = [dot(w, block, 1 - way).astype(BF16) for way, block in ((0, 1), (1, 3))]
        for way in range(2):
            side_out[way, w, 1 - way] = parts[way]
        for way in range(2):
            side(w, way, 1 - way).start()

    def sides_relayed(w):
        parts = [dot(w, block, way) for way, block in ((0, 1), (1, 3))]
        arrived(relay_in.at[:, w], relay_sem.at[w])
        for way in range(2):
            side_out[way, w, way] = (parts[way] + relay_in[way, w].astype(F32)).astype(BF16)
        for way in range(2):
            side(w, way, way).start()

    def finish(w):
        part = dot(w, 0, None)
        arrived(side_in.at[:, w], side_sem.at[w])
        for n in range(2):
            sides = side_in[0, w, n].astype(F32) + side_in[1, w, n].astype(F32)
            total = (part[:, n * HALF : (n + 1) * HALF] + sides).astype(BF16)
            result[w, :, :, n * HALF : (n + 1) * HALF] = total.reshape(CHUNKS, WSTEPS, HALF)
        store(w).start()

    @pl.loop(0, WINDOWS + LAG_0)
    def _(i):
        @pl.when(i < WINDOWS)
        def _():
            make_gated(i)

        for piece, at, blocks in ((0, LAG_2, ()), (1, LAG_2, (2,)), (3, LAG_1, ()), (4, LAG_0, (0,))):

            @pl.when(i == at)
            def _():
                have_weight(piece)
                for block in blocks:
                    have_near_weight(block)

        @pl.when(i == 1)
        def _():
            @pl.loop(0, TILES)
            def _(tile):
                convolve(tile, ((0, tile),), query, EARLY, STEPS // UNROLL)

        @pl.when((i >= LAG_2) & (i < WINDOWS + LAG_2))
        def _():
            w = i - LAG_2
            arrived(gated.at[w, :, pl.ds(0, 2 * WIDTH)], gs_sem.at[w])
            opposite(w)

            @pl.when(w == 0)
            def _():
                have_weight(2)
                have_near_weight(1)
                have_near_weight(3)

            sides_own(w)

        @pl.when((i >= LAG_1) & (i < WINDOWS + LAG_1))
        def _():
            sides_relayed(i - LAG_1)

        @pl.when(i >= LAG_0)
        def _():
            finish(i - LAG_0)

        @pl.when((i >= LAG_F) & (i < WINDOWS + LAG_F))
        def _():
            forward(i - LAG_F).start()

        for piece, at in ((3, 5), (4, 9)):

            @pl.when(i == at)
            def _():
                pass_weight(piece)

    left(halo, HALO)
    for k in range(1, SEQ):

        @pl.when(seq + k < SEQ)
        def _():
            state_copy(k, pl.ds(0, TILES)).wait_send()

    for kind in (WSIB, WZ, WX):
        left(wbuf.at[0], kind)
    left(gated.at[:, :, pl.ds(0, WIDTH)], NEAR)
    left(gated.at[:, :, pl.ds(0, 2 * WIDTH)], SIB)
    left(relay_out, RELAY)
    left(side_out, SIDE)
    pltpu.make_async_copy(result, result, result_sem.at[0]).wait()


def hand_on(source, target, buffer, sems):
    def part(i, into):
        rows = pl.ds(i * SPAN, SPAN)
        if into:
            return pltpu.make_async_copy(source.at[rows], buffer.at[rows], sems.at[0, i])
        return pltpu.make_async_copy(buffer.at[rows], target.at[rows], sems.at[1, i])

    for i in range(ROWS // SPAN):
        part(i, True).start()
    for i in range(ROWS // SPAN):
        part(i, True).wait()
        part(i, False).start()
    for i in range(ROWS // SPAN):
        part(i, False).wait()


def on_device(streams, short_taps, rates, residues, out_weight):
    dma = pltpu.SemaphoreType.DMA
    hbm = pl.BlockSpec(memory_space=pl.ANY)
    result = pl.pallas_call(
        kernel,
        out_shape=jax.ShapeDtypeStruct((CHUNKS, STEPS, WIDTH), BF16),
        in_specs=[hbm] * 5,
        out_specs=hbm,
        scratch_shapes=[
            pltpu.VMEM((3, TAPS, WIDTH), F32),
            pltpu.VMEM((MODES, WIDTH), F32),
            pltpu.VMEM((MODES, WIDTH), F32),
            pltpu.VMEM((3, ROWS, WIDTH), BF16),
            pltpu.VMEM((3, 16, WIDTH), BF16),
            pltpu.VMEM((2 * TILES, CHUNKS * PITCH, LANES), F32),
            pltpu.VMEM((TILES, ROWS, LANES), F32),
            pltpu.VMEM((TILES, ROWS, LANES), F32),
            pltpu.VMEM((TILES, MODES, CHUNKS, LANES), F32),
            pltpu.VMEM((TILES, MODES, CHUNKS, LANES), F32),
            pltpu.VMEM((TILES, MODES, CHUNKS, LANES), F32),
            pltpu.VMEM((TILES, MODES, LANES), F32),
            pltpu.VMEM((SEQ, TILES, MODES, LANES), F32),
            pltpu.VMEM((CHUNKS * SPITCH, LANES), F32),
            pltpu.VMEM((WINDOWS, WROWS, 4 * WIDTH), BF16),
            pltpu.VMEM((4, 4, WIDTH, WIDTH), BF16),
            pltpu.VMEM((2, WINDOWS, WROWS, HALF), BF16),
            pltpu.VMEM((2, WINDOWS, WROWS, HALF), BF16),
            pltpu.VMEM((2, WINDOWS, 2, WROWS, HALF), BF16),
            pltpu.VMEM((2, WINDOWS, 2, WROWS, HALF), BF16),
            pltpu.VMEM((WINDOWS, CHUNKS, WSTEPS, WIDTH), BF16),
            dma((3,)),
            dma((3, TILES)),
            dma((8,)),
            dma((4,)),
            dma((1,)),
            dma((2, SEQ)),
            dma((4,)),
            dma((5,)),
            dma((5,)),
            dma((WINDOWS,)),
            dma((WINDOWS,)),
            dma((WINDOWS,)),
            dma((WINDOWS,)),
            dma((1,)),
        ],
        compiler_params=pltpu.CompilerParams(
            collective_id=0, has_side_effects=True, vmem_limit_bytes=60 * 1024 * 1024
        ),
        cost_estimate=pl.CostEstimate(
            flops=2 * ROWS * WIDTH * 8192, bytes_accessed=16 * 1024 * 1024, transcendentals=0
        ),
        name="mixer",
    )(streams, short_taps, rates.T, residues.T, out_weight)
    return pl.pallas_call(
        hand_on,
        out_shape=jax.ShapeDtypeStruct((ROWS, WIDTH), BF16),
        in_specs=[hbm],
        out_specs=hbm,
        scratch_shapes=[pltpu.VMEM((ROWS, WIDTH), BF16), dma((2, ROWS // SPAN))],
        cost_estimate=pl.CostEstimate(flops=0, bytes_accessed=4 * ROWS * WIDTH, transcendentals=0),
        name="hand_on",
    )(result.reshape(ROWS, WIDTH))


def solution(mesh):
    return jax.shard_map(
        on_device,
        mesh=mesh,
        in_specs=(
            P(None, "seq", "chan"),
            P(None, None, "chan"),
            P("chan", None),
            P("chan", None),
            P("chan", None),
        ),
        out_specs=P("seq", "chan"),
        check_vma=False,
    )
```

```python
import functools

import jax
import jax.numpy as jnp
from jax import lax
from jax.experimental import pallas as pl
from jax.experimental.pallas import tpu as pltpu
from jax.sharding import PartitionSpec as P

MESH = pl.DeviceIdType.MESH
F32 = jnp.float32
BF16 = jnp.bfloat16

TAPS = 7
MODES = 16
ROWS = 2048
WIDTH = 512
LANES = 128
TILES = WIDTH // LANES
CHUNKS = 8
STEPS = ROWS // CHUNKS
WINDOWS = 16
WSTEPS = STEPS // WINDOWS
WROWS = ROWS // WINDOWS
HALF = WIDTH // 2
UNROLL = 16
SPAN = 512
EARLY = 4
PAD = 8
PITCH = STEPS + PAD
SPITCH = WSTEPS + PAD
PIECES = (((2, 0),), ((2, 1),), ((1, 1), (3, 0)), ((1, 0), (3, 1)), ((0, None),))
SEQ = 8
XPART = WIDTH // 4

LAG_F, LAG_2, LAG_1, LAG_0 = 2, 3, 9, 13


def kernel(
    streams, taps_in, rates_in, residues_in, weight, out,
    taps, rates, residues,
    sbuf, halo, nat, prod, query, state, decay, gain, total, totals, stage,
    gated, wbuf, relay_out, relay_in, side_out, side_in, result,
    small_sem, load_sem, out_sem, wown_sem, halo_sem, state_sem, wsib_sem, wz_sem, wx_sem,
    gz_sem, gs_sem, relay_sem, side_sem, result_sem,
):
    seq, chan = lax.axis_index("seq"), lax.axis_index("chan")
    x, zh = lax.div(seq, 2), lax.rem(seq, 2)
    y, zl, core = lax.div(chan, 4), lax.rem(lax.div(chan, 2), 2), lax.rem(chan, 2)
    mine = zl * 2 + core
    sib_chan = chan + 1 - 2 * core
    z_chan = chan + 2 - 4 * zl

    def chan_of(yy, zz, cc):
        return (yy * 2 + zz) * 2 + cc

    def y_off(k):
        return lax.rem(y + k, 4)

    sibling = (seq, sib_chan)
    z_near = (seq, z_chan)
    near = tuple((seq, chan_of(y, 1 - zl, c)) for c in range(2))
    zh_seq = seq + 1 - 2 * zh
    z_far = tuple((zh_seq, chan_of(y, 1 - zl, c)) for c in range(2))
    y_up = (seq, chan_of(y_off(1), zl, core))
    y_down = (seq, chan_of(y_off(3), zl, core))
    x_up = (lax.rem(seq + 2, SEQ), chan)
    x_down = (lax.rem(seq + 6, SEQ), chan)
    seq_of = lambda k: (lax.rem(seq + k, SEQ), chan)

    (HALO, WSIB, WZ, WX, NEAR, SIB, RELAY, SIDE) = range(8)

    def send(src, dst, kind, sem, device):
        return pltpu.make_async_remote_copy(
            src_ref=src, dst_ref=dst, send_sem=out_sem.at[kind], recv_sem=sem,
            device_id=device, device_id_type=MESH,
        )

    def arrived(ref, sem):
        send(ref, ref, 0, sem, sibling).wait_recv()

    def left(ref, kind):
        send(ref, ref, kind, halo_sem.at[0], sibling).wait_send()

    small = [
        pltpu.make_async_copy(a, b, small_sem.at[i])
        for i, (a, b) in enumerate(((rates_in, rates), (residues_in, residues), (taps_in, taps)))
    ]

    def load(j, tile):
        lanes = pl.ds(pl.multiple_of(tile * LANES, LANES), LANES)
        return pltpu.make_async_copy(streams.at[j, :, lanes], sbuf.at[j, :, lanes], load_sem.at[j, tile])

    def columns(block, n, zz, cc):
        first = chan_of(y_off(block), zz, cc) * WIDTH
        if n is None:
            return pl.ds(pl.multiple_of(first, WIDTH), WIDTH)
        return pl.ds(pl.multiple_of(first + n * HALF, HALF), HALF)

    def half(n):
        return slice(None) if n is None else pl.ds(n * HALF, HALF)

    def own_weight(block):
        return pltpu.make_async_copy(
            weight.at[:, columns(block, None, zl, core)], wbuf.at[block, mine], wown_sem.at[block]
        )

    barrier = pltpu.get_barrier_semaphore()
    partners = [seq_of(k) for k in range(1, SEQ)] + [sibling, *near, *z_far, y_up, y_down]
    for device in partners:
        pl.semaphore_signal(barrier, inc=1, device_id=device, device_id_type=MESH)
    for copy in small:
        copy.start()
    for tile in range(TILES):
        for j in (1, 2):
            load(j, tile).start()

    halo_copy = send(streams.at[:, pl.ds(ROWS - 16, 16)], halo, HALO, halo_sem.at[0], seq_of(1))

    pair = 2 * lax.rem(x, 2)
    far_sources = pl.ds(2 - 2 * zl, 2)

    def part_rows(part):
        return pl.ds(pl.multiple_of(part * XPART, XPART), XPART)

    def piece_rows(piece):
        return HALF if piece < 2 else WIDTH

    def start_weight(piece):
        for block, n in PIECES[piece]:
            for link in range(2):
                chip = near if link == 1 and piece < 3 else z_far
                for c in range(2):
                    send(
                        weight.at[part_rows(pair + link), columns(block, n, 1 - zl, c)],
                        wbuf.at[block, mine, part_rows(pair + link), half(n)],
                        WZ, wz_sem.at[piece], chip[c],
                    ).start()

    def pass_weight(piece):
        arrived(wbuf.at[0, 0, pl.ds(0, piece_rows(piece))], wz_sem.at[piece])
        for block, n in PIECES[piece]:
            for way, device in enumerate((x_up, x_down)):
                there = wbuf.at[block, far_sources, part_rows(pair + way), half(n)]
                send(there, there, WX, wx_sem.at[piece], device).start()

    def have_weight(piece):
        arrived(wbuf.at[0, 0, pl.ds(0, piece_rows(piece))], wx_sem.at[piece])

    def near_weight(block):
        there = wbuf.at[block, mine]
        return send(weight.at[:, columns(block, None, zl, 1 - core)], there, WSIB, wsib_sem.at[block], sibling)

    def have_near_weight(block):
        arrived(wbuf.at[block, 0], wsib_sem.at[block])
        own_weight(block).wait()

    pl.semaphore_wait(barrier, len(partners))
    halo_copy.start()
    start_weight(0)
    for copy in small:
        copy.wait()

    def lanes_of(tile):
        return pl.ds(pl.multiple_of(tile * LANES, LANES), LANES)

    @pl.loop(0, TILES)
    def _(tile):
        rate = rates[:, lanes_of(tile)]
        slope = jnp.tanh(rate)
        scale = residues[:, lanes_of(tile)] * jnp.sqrt(2.0 * slope / (1.0 + slope))
        kept = jnp.exp(-rate)
        for m in range(MODES):
            decay[tile, m] = jnp.broadcast_to(kept[m : m + 1], (CHUNKS, LANES))
            gain[tile, m] = jnp.broadcast_to(scale[m : m + 1], (CHUNKS, LANES))

    first = jnp.where(seq > 0, 1.0, 0.0).astype(F32)

    def edge(j, tile, slot):
        nat[slot, pl.ds(0, PAD)] = halo[j, :, lanes_of(tile)].astype(F32)[16 - PAD :] * first

    def widen(j, tile, slot):
        lanes = lanes_of(tile)
        nat[slot, pl.ds(PAD, STEPS)] = sbuf[j, pl.ds(0, STEPS), lanes].astype(F32)

        @pl.loop(1, CHUNKS)
        def _(c):
            row = pl.multiple_of(c * STEPS - 16, 16)
            to = pl.multiple_of(c * PITCH, PAD)
            nat[slot, pl.ds(to, PITCH)] = sbuf[j, pl.ds(row, STEPS + 16), lanes].astype(F32)[16 - PAD :]

    def across(slot, step):
        return nat[slot, pl.ds(PAD + step, CHUNKS, stride=PITCH), :]

    def filtered(window, coefs):
        terms = [c * v for c, v in zip(coefs, window, strict=True)]
        while len(terms) > 1:
            terms = [a + b for a, b in zip(terms[::2], terms[1::2])] + ([terms[-1]] if len(terms) % 2 else [])
        return terms[0]

    def coefs_of(j, tile):
        return [
            jnp.broadcast_to(taps[j, pl.ds(i, 1), lanes_of(tile)], (CHUNKS, LANES)) for i in range(TAPS)
        ]

    def convolve(tile, pairs, target, first_group, groups):
        coefs = [coefs_of(j, tile) for j, _ in pairs]
        before = [tuple(across(slot, first_group * UNROLL - i) for i in range(1, TAPS)) for _, slot in pairs]

        def body(g, before):
            before = list(before)
            for u in range(UNROLL):
                step = g * UNROLL + u
                value = None
                for k, (_, slot) in enumerate(pairs):
                    window = (across(slot, step), *before[k])
                    part = filtered(window, coefs[k])
                    value = part if value is None else value * part
                    before[k] = window[:-1]
                target[tile, pl.ds(pl.multiple_of(step * CHUNKS, CHUNKS), CHUNKS)] = value
            return tuple(before)

        lax.fori_loop(first_group, groups, body, tuple(before))

    @pl.loop(0, TILES)
    def _(tile):
        load(1, tile).wait()
        load(2, tile).wait()
        widen(1, tile, 2 * tile)
        widen(2, tile, 2 * tile + 1)

        for slot in range(2):
            nat[2 * tile + slot, pl.ds(0, PAD)] = jnp.zeros((PAD, LANES), F32)
        convolve(tile, ((1, 2 * tile), (2, 2 * tile + 1)), prod, 0, STEPS // UNROLL)

        @pl.when(tile == 0)
        def _():
            start_weight(1)

        @pl.when(tile == 2)
        def _():
            pass_weight(0)

        @pl.when(tile == 2)
        def _():
            start_weight(2)
            for block in (2, 1, 3, 0):
                near_weight(block).start()
                own_weight(block).start()

    for tile in range(TILES):
        load(0, tile).start()
    arrived(halo, halo_sem.at[0])

    @pl.loop(0, TILES)
    def _(tile):
        edge(1, tile, 2 * tile)
        edge(2, tile, 2 * tile + 1)
        convolve(tile, ((1, 2 * tile), (2, 2 * tile + 1)), prod, 0, 1)

    def state_copy(k, tiles):
        return pltpu.make_async_remote_copy(
            src_ref=total.at[tiles], dst_ref=totals.at[k, tiles],
            send_sem=state_sem.at[0, k], recv_sem=state_sem.at[1, k],
            device_id=seq_of(k), device_id_type=MESH,
        )

    for k in range(1, SEQ):

        @pl.when(seq < k)
        def _():
            totals[k] = jnp.zeros((TILES, MODES, LANES), F32)

    sublane = lax.broadcasted_iota(jnp.int32, (CHUNKS, LANES), 0)

    @pl.loop(0, TILES)
    def _(tile):
        decays = [decay[tile, m] for m in range(MODES)]

        def body(g, states):
            states = list(states)
            for u in range(UNROLL):
                step = pl.multiple_of((g * UNROLL + u) * CHUNKS, CHUNKS)
                value = prod[tile, pl.ds(step, CHUNKS)]
                states = [a * s + value for a, s in zip(decays, states)]
            return tuple(states)

        zero = jnp.zeros((CHUNKS, LANES), F32)
        ends = lax.fori_loop(0, STEPS // UNROLL, body, (zero,) * MODES)
        for m in range(MODES):
            rate = jnp.broadcast_to(rates[pl.ds(m, 1), lanes_of(tile)], (CHUNKS, LANES))
            run = ends[m]
            for shift in (1, 2, 4):
                moved = jnp.where(sublane >= shift, pltpu.roll(run, shift, 0), 0.0)
                run = run + jnp.exp(-rate * float(STEPS * shift)) * moved
            state[tile, m] = jnp.where(sublane >= 1, pltpu.roll(run, 1, 0), 0.0)
            total[tile, pl.ds(m, 1)] = run[CHUNKS - 1 :]

        for k in range(1, SEQ):

            @pl.when(seq + k < SEQ)
            def _():
                state_copy(k, pl.ds(tile, 1)).start()

        @pl.when(tile == 0)
        def _():
            pass_weight(1)


    @pl.loop(0, TILES)
    def _(tile):
        load(0, tile).wait()
        widen(0, tile, tile)
        edge(0, tile, tile)
        convolve(tile, ((0, tile),), query, 0, EARLY)

    start_weight(3)
    pass_weight(2)
    for k in range(1, SEQ):

        @pl.when(seq >= k)
        def _():
            state_copy(k, pl.ds(0, TILES)).wait_recv()

    @pl.loop(0, TILES)
    def _(tile):
        rate = rates[:, lanes_of(tile)]
        start = jnp.zeros((MODES, LANES), F32)
        for k in range(1, SEQ):
            part = jnp.exp(-rate * float(ROWS * (k - 1))) * totals[k, tile]
            start = start + jnp.where(seq >= k, part, 0.0)
        for m in range(MODES):
            spread = jnp.broadcast_to(rate[m : m + 1], (CHUNKS, LANES)) * (sublane * STEPS).astype(F32)
            state[tile, m] = state[tile, m] + jnp.exp(-spread) * start[m : m + 1]

    start_weight(4)
    def own_lanes():
        return pl.ds(pl.multiple_of(mine * WIDTH, WIDTH), WIDTH)

    def part_of(w, source):
        return gated.at[w, :, pl.ds(pl.multiple_of(source * WIDTH, WIDTH), WIDTH)]

    def to_near(w):
        return send(part_of(w, mine), part_of(w, mine), NEAR, gz_sem.at[w], z_near)

    def to_sibling(w):
        return send(part_of(w, mine), part_of(w, mine), SIB, gs_sem.at[w], sibling)

    def forward(w):
        source = (1 - zl) * 2 + core
        arrived(part_of(w, source), gz_sem.at[w])
        return send(part_of(w, source), part_of(w, source), SIB, gs_sem.at[w], sibling)

    def make_gated(w):
        @pl.loop(0, TILES)
        def _(tile):
            decays = [decay[tile, m] for m in range(MODES)]
            weights = [gain[tile, m] for m in range(MODES)]

            def body(g, states):
                states = list(states)
                for u in range(UNROLL):
                    at = g * UNROLL + u
                    row = pl.ds(pl.multiple_of((w * WSTEPS + at) * CHUNKS, CHUNKS), CHUNKS)
                    value = prod[tile, row]
                    states = [a * s + value for a, s in zip(decays, states)]
                    mixed = filtered(states, weights)
                    stage[pl.ds(at, CHUNKS, stride=SPITCH), :] = mixed * query[tile, row]
                return tuple(states)

            states = lax.fori_loop(0, WSTEPS // UNROLL, body, tuple(state[tile, m] for m in range(MODES)))
            for m in range(MODES):
                state[tile, m] = states[m]
            lanes = pl.ds(pl.multiple_of(mine * WIDTH + tile * LANES, LANES), LANES)
            for c in range(CHUNKS):
                rows = pl.ds(c * WSTEPS, WSTEPS)
                gated[w, rows, lanes] = stage[pl.ds(c * SPITCH, WSTEPS)].astype(BF16)

        to_near(w).start()
        to_sibling(w).start()

    def dot(w, block, n):
        columns = wbuf[block, :, :, half(n)]
        return jnp.dot(gated[w], columns.reshape(4 * WIDTH, -1), preferred_element_type=F32)

    ups = (y_up, y_down)

    def side(w, way, n):
        return send(side_out.at[way, w, n], side_in.at[way, w, n], SIDE, side_sem.at[w], ups[way])

    def store(w):
        rows = pl.ds(pl.multiple_of(w * WSTEPS, WSTEPS), WSTEPS)
        return pltpu.make_async_copy(result.at[w], out.at[:, rows], result_sem.at[0])

    def opposite(w):
        part = dot(w, 2, None).astype(BF16)
        for way in range(2):
            relay_out[way, w] = part[:, way * HALF : (way + 1) * HALF]
        for way in range(2):
            send(relay_out.at[way, w], relay_in.at[way, w], RELAY, relay_sem.at[w], ups[way]).start()

    def sides_own(w):
        parts = [dot(w, block, 1 - way).astype(BF16) for way, block in ((0, 1), (1, 3))]
        for way in range(2):
            side_out[way, w, 1 - way] = parts[way]
        for way in range(2):
            side(w, way, 1 - way).start()

    def sides_relayed(w):
        parts = [dot(w, block, way) for way, block in ((0, 1), (1, 3))]
        arrived(relay_in.at[:, w], relay_sem.at[w])
        for way in range(2):
            side_out[way, w, way] = (parts[way] + relay_in[way, w].astype(F32)).astype(BF16)
        for way in range(2):
            side(w, way, way).start()

    def finish(w):
        part = dot(w, 0, None)
        arrived(side_in.at[:, w], side_sem.at[w])
        for n in range(2):
            sides = side_in[0, w, n].astype(F32) + side_in[1, w, n].astype(F32)
            total = (part[:, n * HALF : (n + 1) * HALF] + sides).astype(BF16)
            result[w, :, :, n * HALF : (n + 1) * HALF] = total.reshape(CHUNKS, WSTEPS, HALF)
        store(w).start()

    @pl.loop(0, WINDOWS + LAG_0)
    def _(i):
        @pl.when(i < WINDOWS)
        def _():
            make_gated(i)

        for piece, at, blocks in ((0, LAG_2, ()), (1, LAG_2, (2,)), (3, LAG_1, ()), (4, LAG_0, (0,))):

            @pl.when(i == at)
            def _():
                have_weight(piece)
                for block in blocks:
                    have_near_weight(block)

        @pl.when(i == 1)
        def _():
            @pl.loop(0, TILES)
            def _(tile):
                convolve(tile, ((0, tile),), query, EARLY, STEPS // UNROLL)

        @pl.when((i >= LAG_2) & (i < WINDOWS + LAG_2))
        def _():
            w = i - LAG_2
            arrived(gated.at[w, :, pl.ds(0, 2 * WIDTH)], gs_sem.at[w])
            opposite(w)

            @pl.when(w == 0)
            def _():
                have_weight(2)
                have_near_weight(1)
                have_near_weight(3)

            sides_own(w)

        @pl.when((i >= LAG_1) & (i < WINDOWS + LAG_1))
        def _():
            sides_relayed(i - LAG_1)

        @pl.when(i >= LAG_0)
        def _():
            finish(i - LAG_0)

        @pl.when((i >= LAG_F) & (i < WINDOWS + LAG_F))
        def _():
            forward(i - LAG_F).start()

        for piece, at in ((3, 5), (4, 9)):

            @pl.when(i == at)
            def _():
                pass_weight(piece)

    left(halo, HALO)
    for k in range(1, SEQ):

        @pl.when(seq + k < SEQ)
        def _():
            state_copy(k, pl.ds(0, TILES)).wait_send()

    for kind in (WSIB, WZ, WX):
        left(wbuf.at[0], kind)
    left(gated.at[:, :, pl.ds(0, WIDTH)], NEAR)
    left(gated.at[:, :, pl.ds(0, 2 * WIDTH)], SIB)
    left(relay_out, RELAY)
    left(side_out, SIDE)
    pltpu.make_async_copy(result, result, result_sem.at[0]).wait()


def hand_on(source, target, buffer, sems):
    def part(i, into):
        rows = pl.ds(i * SPAN, SPAN)
        if into:
            return pltpu.make_async_copy(source.at[rows], buffer.at[rows], sems.at[0, i])
        return pltpu.make_async_copy(buffer.at[rows], target.at[rows], sems.at[1, i])

    for i in range(ROWS // SPAN):
        part(i, True).start()
    for i in range(ROWS // SPAN):
        part(i, True).wait()
        part(i, False).start()
    for i in range(ROWS // SPAN):
        part(i, False).wait()


def on_device(streams, short_taps, rates, residues, out_weight):
    dma = pltpu.SemaphoreType.DMA
    hbm = pl.BlockSpec(memory_space=pl.ANY)
    result = pl.pallas_call(
        kernel,
        out_shape=jax.ShapeDtypeStruct((CHUNKS, STEPS, WIDTH), BF16),
        in_specs=[hbm] * 5,
        out_specs=hbm,
        scratch_shapes=[
            pltpu.VMEM((3, TAPS, WIDTH), F32),
            pltpu.VMEM((MODES, WIDTH), F32),
            pltpu.VMEM((MODES, WIDTH), F32),
            pltpu.VMEM((3, ROWS, WIDTH), BF16),
            pltpu.VMEM((3, 16, WIDTH), BF16),
            pltpu.VMEM((2 * TILES, (CHUNKS + 1) * PITCH, LANES), F32),
            pltpu.VMEM((TILES, ROWS, LANES), F32),
            pltpu.VMEM((TILES, ROWS, LANES), F32),
            pltpu.VMEM((TILES, MODES, CHUNKS, LANES), F32),
            pltpu.VMEM((TILES, MODES, CHUNKS, LANES), F32),
            pltpu.VMEM((TILES, MODES, CHUNKS, LANES), F32),
            pltpu.VMEM((TILES, MODES, LANES), F32),
            pltpu.VMEM((SEQ, TILES, MODES, LANES), F32),
            pltpu.VMEM(((CHUNKS + 1) * SPITCH, LANES), F32),
            pltpu.VMEM((WINDOWS, WROWS, 4 * WIDTH), BF16),
            pltpu.VMEM((4, 4, WIDTH, WIDTH), BF16),
            pltpu.VMEM((2, WINDOWS, WROWS, HALF), BF16),
            pltpu.VMEM((2, WINDOWS, WROWS, HALF), BF16),
            pltpu.VMEM((2, WINDOWS, 2, WROWS, HALF), BF16),
            pltpu.VMEM((2, WINDOWS, 2, WROWS, HALF), BF16),
            pltpu.VMEM((WINDOWS, CHUNKS, WSTEPS, WIDTH), BF16),
            dma((3,)),
            dma((3, TILES)),
            dma((8,)),
            dma((4,)),
            dma((1,)),
            dma((2, SEQ)),
            dma((4,)),
            dma((5,)),
            dma((5,)),
            dma((WINDOWS,)),
            dma((WINDOWS,)),
            dma((WINDOWS,)),
            dma((WINDOWS,)),
            dma((1,)),
        ],
        compiler_params=pltpu.CompilerParams(
            collective_id=0, has_side_effects=True, vmem_limit_bytes=60 * 1024 * 1024
        ),
        cost_estimate=pl.CostEstimate(
            flops=2 * ROWS * WIDTH * 8192, bytes_accessed=16 * 1024 * 1024, transcendentals=0
        ),
        name="mixer",
    )(streams, short_taps, rates.T, residues.T, out_weight)
    return pl.pallas_call(
        hand_on,
        out_shape=jax.ShapeDtypeStruct((ROWS, WIDTH), BF16),
        in_specs=[hbm],
        out_specs=hbm,
        scratch_shapes=[pltpu.VMEM((ROWS, WIDTH), BF16), dma((2, ROWS // SPAN))],
        cost_estimate=pl.CostEstimate(flops=0, bytes_accessed=4 * ROWS * WIDTH, transcendentals=0),
        name="hand_on",
    )(result.reshape(ROWS, WIDTH))


def solution(mesh):
    return jax.shard_map(
        on_device,
        mesh=mesh,
        in_specs=(
            P(None, "seq", "chan"),
            P(None, None, "chan"),
            P("chan", None),
            P("chan", None),
            P("chan", None),
        ),
        out_specs=P("seq", "chan"),
        check_vma=False,
    )
```
